32 devices in a mesh: az: 16 (over z, y, core), mer: 2 (over x).
Axes of the slice: x: 2, y: 2, z: 4, core: 2. Of those that a mesh axis runs over, the one named last changes fastest.
Arguments:
- velocity_modes: bfloat16 [3, 1024, 4096], P(None, 'az', 'mer'), may hold values from -6 to 6
- geometry: float32 [3, 128, 32], P(None, 'az', 'mer'), may hold values from 0.5 to 2
- derivative: float32 [2, 8, 8], replicated, may hold values from -2 to 2
- blade_load: bfloat16 [16, 3, 3, 1024], P('az'), may hold values from -6 to 6
- blade_owner: int32 [36], replicated, may hold values from 0 to 47, as said below
- spread_tile: int32 [2, 16, 4], P('mer', 'az'), may hold values from 0 to 287
- spread_azimuth: bfloat16 [2, 16, 4, 128, 1024], P('mer', 'az'), may hold values from -1.25 to 1.25
- spread_meridional: bfloat16 [2, 16, 4, 128, 128], P('mer', 'az'), may hold values from -1.25 to 1.25
Outputs:
- term_modes: bfloat16 [3, 1024, 4096], P(None, 'az', 'mer')
The draws below stay inside these ranges and needn't reach their ends.
Inputs may be any that keep to these rules, and one draw needn't show every extreme that they name: Distinct values; blade_owner includes 0 and 47.
All inputs are finite; a program needn't handle non-finite values.
Results may differ from the reference program's by a relative error of at most 0.0073.
Values may be sent and summed in bfloat16 or wider, within the bound.
A program may use at most 64 MiB of HBM per device.

```python
import math
import jax
import jax.numpy as jnp
from jax import lax

PLANES = 1024
RB = 8
CZ = 16
BLADES = 36
MARK = 1024
TILE = 128
JOBS = 4
TILES = 8
SLOTS = 3
SLOTS_ALL = 48
NR = 128
NZ = 32
NODES = 4096
N_AZ = 16
N_MER = 2


def draw_blade_owner(key, part):
    key = jax.random.fold_in(key, 11)
    key_mid, key_order = jax.random.split(key)
    middle = 1 + jax.random.permutation(key_mid, SLOTS_ALL - 2)[:BLADES - 2]
    values = jnp.concatenate([jnp.zeros((1,), jnp.int32), middle.astype(jnp.int32), jnp.full((1,), SLOTS_ALL - 1, jnp.int32)])
    order = jax.random.permutation(key_order, BLADES)
    return values[order].astype(jnp.int32)


def set_ends(entries, own_key, least, high):
    longest = entries.shape.index(max(entries.shape))
    spots = []
    for shift in (0, 1):
        where = [jax.random.randint(jax.random.fold_in(own_key, axis), (), 0, length) for axis, length in enumerate(entries.shape)]
        where[longest] = (where[longest] + shift) % entries.shape[longest]
        spots.append(tuple(where))
    return entries.at[spots[0]].set(least).at[spots[1]].set(high)


def shard_levels(rng, shape, cuts, low, high):
    factor_of = 1.0
    for position, blocks in cuts:
        draws = jax.random.uniform(jax.random.fold_in(jax.random.fold_in(rng, 6), position), (blocks,), jnp.float32, low / len(cuts), high / len(cuts))
        factor_of = factor_of * jnp.repeat(jnp.exp(draws), shape[position] // blocks).reshape((-1,) + (1,) * (len(shape) - 1 - position))
    return factor_of


def bell_draw(key, shape, deviation, most, shards=(), held_as=jnp.bfloat16):
    drawn = jax.random.normal(key, shape, jnp.float32) * deviation
    if len(shards) > 0:
        drawn = shard_levels(key, shape, shards, -0.22, 0.18) * drawn
    return jnp.clip(drawn, min=-most, max=most).astype(held_as)


def setup_inputs(seed: int = 0) -> dict:
    streams_of = jax.random.split(jax.random.key(seed), 9)
    return {
        "velocity_modes": bell_draw(streams_of[0], (3, PLANES, NODES), 1.0, 6.0, ((1, 16), (2, 2))),
        "geometry": jnp.clip(0.5 + 1.5 * jax.random.uniform(streams_of[1], (3, NR, NZ), jnp.float32) ** shard_levels(streams_of[1], (3, NR, NZ), ((1, 16), (2, 2)), -0.2, 0.2), 0.5, 2.0),
        "derivative": bell_draw(streams_of[2], (2, RB, RB), RB ** -0.5, 2.0, (), jnp.float32),
        "blade_load": bell_draw(streams_of[3], (N_AZ, SLOTS, 3, MARK), 1.0, 6.0, ((0, 16),)),
        "blade_owner": draw_blade_owner(jax.random.fold_in(streams_of[8], 71), 0),
        "spread_tile": set_ends(jax.random.randint(streams_of[5], (N_MER, N_AZ, JOBS), 0, BLADES * TILES), jax.random.fold_in(streams_of[5], 1), 0, (BLADES * TILES) - 1).astype(jnp.int32),
        "spread_azimuth": bell_draw(streams_of[6], (N_MER, N_AZ, JOBS, TILE, PLANES), 24 ** -0.5, 1.25, ((0, 2), (1, 16))),
        "spread_meridional": bell_draw(streams_of[7], (N_MER, N_AZ, JOBS, TILE, RB * CZ), 24 ** -0.5, 1.25, ((0, 2), (1, 16))),
    }


def make_table(planes):
    row_index = jnp.arange(planes, dtype=jnp.int32)
    wave_index = row_index // 2
    phase_index = row_index[:, None] * wave_index[None, :] % planes
    angle_rad = phase_index.astype(jnp.float32) * (2.0 * math.pi / planes)
    even_rows = (row_index % 2 == 0)[None, :]
    dft_table = math.sqrt(2.0 / planes) * jnp.where(even_rows, jnp.cos(angle_rad), -jnp.sin(angle_rad))
    return dft_table.astype(jnp.bfloat16)

def slope_of(mode_block, first_pair, planes):
    shape_all = mode_block.shape
    mode_pairs = mode_block.reshape(shape_all[0], shape_all[1] // 2, 2, shape_all[2]).astype(jnp.float32)
    wave_number = (first_pair + jnp.arange(shape_all[1] // 2, dtype=jnp.int32)).astype(jnp.float32) * (2.0 * math.pi / planes)
    wave_number = wave_number[None, :, None]
    result = jnp.stack([-wave_number * mode_pairs[:, :, 1], wave_number * mode_pairs[:, :, 0]], axis=2)
    return result.reshape(shape_all).astype(jnp.bfloat16)

def inverse_of(dft_table, mode_block):
    return jnp.einsum('pj,cjn->cpn', dft_table, mode_block, preferred_element_type=jnp.float32)

def slopes_of(velocity, geometry, derivative):
    hp = lax.Precision.HIGHEST
    shape_all = velocity.shape
    elem_size = derivative.shape[1]
    elements = shape_all[3] // elem_size
    radial_slope = geometry[1] * jnp.einsum('rs,cpsz->cprz', derivative[0], velocity, precision=hp)
    blocks = velocity.reshape(shape_all[0], shape_all[1], shape_all[2], elements, elem_size)
    raw_slope = jnp.einsum('at,cpret->cprea', derivative[1], blocks, precision=hp)
    axial_slope = raw_slope * geometry[2].reshape(shape_all[2], elements, elem_size)
    first_face = axial_slope[..., 0]
    last_face = axial_slope[..., elem_size - 1]
    face_mean = 0.5 * (last_face[..., :-1] + first_face[..., 1:])
    new_first = first_face.at[..., 1:].set(face_mean)
    new_last = last_face.at[..., :-1].set(face_mean)
    return (radial_slope, axial_slope, first_face, last_face, new_first, new_last)

def advect(velocity, radial_slope, axial_slope, swirl_slope, inverse_radius):
    radial_vel = velocity[0]
    swirl_vel = velocity[1]
    axial_vel = velocity[2]
    advection = radial_vel[None] * radial_slope + axial_vel[None] * axial_slope + (inverse_radius * swirl_vel)[None] * swirl_slope
    advection = advection.at[0].add(-(inverse_radius * swirl_vel * swirl_vel))
    advection = advection.at[1].add(inverse_radius * radial_vel * swirl_vel)
    return advection

def forcing_of(all_loads, tile_ids, spread_az, spread_mer, tile_size):
    blades = all_loads.shape[0]
    tiles_count = all_loads.shape[2] // tile_size
    tile_loads = all_loads.reshape(blades, 3, tiles_count, tile_size).transpose(0, 2, 1, 3).reshape(blades * tiles_count, 3, tile_size)
    picked = jnp.take(tile_loads, tile_ids, axis=0)
    scaled = (picked.astype(jnp.float32)[:, :, :, None] * spread_mer.astype(jnp.float32)[:, None, :, :]).astype(jnp.bfloat16)
    return jnp.einsum('jmp,jcmn->cpn', spread_az, scaled, preferred_element_type=jnp.float32)

def reference(velocity_modes, geometry, derivative, blade_load, blade_owner, spread_tile, spread_azimuth, spread_meridional):
    dft_table = make_table(PLANES)
    all_loads = blade_load.reshape(N_AZ * SLOTS, 3, MARK)[blade_owner]
    shaped = velocity_modes.reshape(3, PLANES, N_MER, NR, CZ)

    def one_block(block_index):
        part = lax.dynamic_slice_in_dim(shaped, block_index * RB, RB, 3)
        mode_block = part.transpose(0, 1, 3, 2, 4).reshape(3, PLANES, RB * NZ)
        slope_block = slope_of(mode_block, jnp.int32(0), PLANES)
        velocity = inverse_of(dft_table, mode_block).reshape(3, PLANES, RB, NZ)
        swirl_slope = inverse_of(dft_table, slope_block).reshape(3, PLANES, RB, NZ)
        geo = lax.dynamic_slice_in_dim(geometry, block_index * RB, RB, 1)
        radial_slope, axial_slope, first_face, last_face, new_first, new_last = slopes_of(velocity, geo, derivative)
        axial_slope = axial_slope.at[..., 0].set(new_first).at[..., RB - 1].set(new_last)
        axial_slope = axial_slope.reshape(3, PLANES, RB, NZ)
        advection = advect(velocity, radial_slope, axial_slope, swirl_slope, geo[0])
        pieces = []
        for mer_index in range(N_MER):
            force = forcing_of(all_loads, spread_tile[mer_index][block_index], spread_azimuth[mer_index][block_index], spread_meridional[mer_index][block_index], TILE)
            pieces.append(force.reshape(3, PLANES, RB, CZ))
        forcing = jnp.concatenate(pieces, axis=3)
        total_term = (advection + forcing).astype(jnp.bfloat16).reshape(3, PLANES, RB * NZ)
        result = jnp.einsum('pj,cpn->cjn', dft_table, total_term, preferred_element_type=jnp.float32).astype(jnp.bfloat16)
        return result.reshape(3, PLANES, RB, N_MER, CZ)
    stacked = lax.map(one_block, jnp.arange(N_AZ, dtype=jnp.int32))
    return stacked.transpose(1, 2, 4, 0, 3, 5).reshape(3, PLANES, NODES)
```

```python
import functools
import math

import jax
import jax.numpy as jnp
import ml_dtypes
import numpy as np
from jax import lax
from jax.experimental import pallas as pl
from jax.experimental.pallas import tpu as pltpu
from jax.sharding import PartitionSpec as P

PLANES = 1024
TILE = 128


def extended(shard, sides, width):
    for axis, dim in sides:
        count, length = (lax.axis_size(axis), shard.shape[dim])
        up = [(i, (i + 1) % count) for i in range(count - 1)]
        down = [(j, i) for i, j in up]
        last = lax.slice_in_dim(shard, length - width, length, axis=dim)
        leading = lax.slice_in_dim(shard, 0, width, axis=dim)
        before = lax.ppermute(last, axis, up)
        after = lax.ppermute(leading, axis, down)
        shard = jnp.concatenate([before, shard, after], axis=dim)
    return shard


def make_table(planes):
    row_index = jnp.arange(planes, dtype=jnp.int32)
    wave_index = row_index // 2
    phase_index = row_index[:, None] * wave_index[None, :] % planes
    angle_rad = phase_index.astype(jnp.float32) * (2.0 * math.pi / planes)
    even_rows = (row_index % 2 == 0)[None, :]
    dft_table = math.sqrt(2.0 / planes) * jnp.where(
        even_rows, jnp.cos(angle_rad), -jnp.sin(angle_rad)
    )
    return dft_table.astype(jnp.bfloat16)


def slope_of(mode_block, first_pair, planes):
    shape_all = mode_block.shape
    mode_pairs = mode_block.reshape(shape_all[0], shape_all[1] // 2, 2, shape_all[2]).astype(
        jnp.float32
    )
    wave_number = (first_pair + jnp.arange(shape_all[1] // 2, dtype=jnp.int32)).astype(
        jnp.float32
    ) * (2.0 * math.pi / planes)
    wave_number = wave_number[None, :, None]
    result = jnp.stack(
        [-wave_number * mode_pairs[:, :, 1], wave_number * mode_pairs[:, :, 0]], axis=2
    )
    return result.reshape(shape_all).astype(jnp.bfloat16)


def inverse_of(dft_table, mode_block):
    return jnp.einsum("pj,cjn->cpn", dft_table, mode_block, preferred_element_type=jnp.float32)


def slopes_of(velocity, geometry, derivative):
    hp = lax.Precision.HIGHEST
    shape_all = velocity.shape
    elem_size = derivative.shape[1]
    elements = shape_all[3] // elem_size
    radial_slope = geometry[1] * jnp.einsum("rs,cpsz->cprz", derivative[0], velocity, precision=hp)
    blocks = velocity.reshape(shape_all[0], shape_all[1], shape_all[2], elements, elem_size)
    raw_slope = jnp.einsum("at,cpret->cprea", derivative[1], blocks, precision=hp)
    axial_slope = raw_slope * geometry[2].reshape(shape_all[2], elements, elem_size)
    first_face = axial_slope[..., 0]
    last_face = axial_slope[..., elem_size - 1]
    face_mean = 0.5 * (last_face[..., :-1] + first_face[..., 1:])
    new_first = first_face.at[..., 1:].set(face_mean)
    new_last = last_face.at[..., :-1].set(face_mean)
    return (radial_slope, axial_slope, first_face, last_face, new_first, new_last)


def advect(velocity, radial_slope, axial_slope, swirl_slope, inverse_radius):
    radial_vel = velocity[0]
    swirl_vel = velocity[1]
    axial_vel = velocity[2]
    advection = (
        radial_vel[None] * radial_slope
        + axial_vel[None] * axial_slope
        + (inverse_radius * swirl_vel)[None] * swirl_slope
    )
    advection = advection.at[0].add(-(inverse_radius * swirl_vel * swirl_vel))
    advection = advection.at[1].add(inverse_radius * radial_vel * swirl_vel)
    return advection


def forcing_of(all_loads, tile_ids, spread_az, spread_mer, tile_size):
    blades = all_loads.shape[0]
    tiles_count = all_loads.shape[2] // tile_size
    tile_loads = (
        all_loads.reshape(blades, 3, tiles_count, tile_size)
        .transpose(0, 2, 1, 3)
        .reshape(blades * tiles_count, 3, tile_size)
    )
    picked = jnp.take(tile_loads, tile_ids, axis=0)
    scaled = (
        picked.astype(jnp.float32)[:, :, :, None] * spread_mer.astype(jnp.float32)[:, None, :, :]
    ).astype(jnp.bfloat16)
    return jnp.einsum("jmp,jcmn->cpn", spread_az, scaled, preferred_element_type=jnp.float32)


def on_device(
    velocity_modes,
    geometry,
    derivative,
    blade_load,
    blade_owner,
    spread_tile,
    spread_azimuth,
    spread_meridional,
):
    planes = PLANES
    dft_table = make_table(planes)
    local_modes = velocity_modes.shape[1]
    block_cells = geometry.shape[1] * geometry.shape[2]
    first_pair = lax.axis_index("az") * (local_modes // 2)
    slope_local = slope_of(velocity_modes, first_pair, planes)
    velocity = inverse_of(
        dft_table, lax.all_to_all(velocity_modes, "az", split_axis=2, concat_axis=1, tiled=True)
    )
    swirl_slope = inverse_of(
        dft_table, lax.all_to_all(slope_local, "az", split_axis=2, concat_axis=1, tiled=True)
    )
    rows = geometry.shape[1]
    cells = geometry.shape[2]
    velocity = velocity.reshape(3, planes, rows, cells)
    swirl_slope = swirl_slope.reshape(3, planes, rows, cells)
    radial_slope, axial_slope, first_face, last_face, new_first, new_last = slopes_of(
        velocity, geometry, derivative
    )
    edge_values = jnp.stack([first_face[..., 0], last_face[..., -1]], axis=-1)
    padded = extended(edge_values.astype(jnp.bfloat16), (("mer", 3),), 1).astype(edge_values.dtype)
    mer_index = lax.axis_index("mer")
    mer_count = lax.axis_size("mer")
    left_value = jnp.where(
        mer_index > 0, 0.5 * (padded[..., 0] + first_face[..., 0]), first_face[..., 0]
    )
    right_value = jnp.where(
        mer_index < mer_count - 1, 0.5 * (last_face[..., -1] + padded[..., 3]), last_face[..., -1]
    )
    new_first = new_first.at[..., 0].set(left_value)
    new_last = new_last.at[..., -1].set(right_value)
    elem_size = derivative.shape[1]
    axial_slope = axial_slope.at[..., 0].set(new_first).at[..., elem_size - 1].set(new_last)
    axial_slope = axial_slope.reshape(3, planes, rows, cells)
    advection = advect(velocity, radial_slope, axial_slope, swirl_slope, geometry[0])
    local_slots = blade_load[0]
    every_slot = lax.all_gather(blade_load, "az", axis=0, tiled=True)
    all_loads = every_slot.reshape(-1, 3, local_slots.shape[2])[blade_owner]
    forcing = forcing_of(
        all_loads, spread_tile[0, 0], spread_azimuth[0, 0], spread_meridional[0, 0], TILE
    )
    total_term = (advection.reshape(3, planes, block_cells) + forcing).astype(jnp.bfloat16)
    result = jnp.einsum(
        "pj,cpn->cjn", dft_table, total_term, preferred_element_type=jnp.float32
    ).astype(jnp.bfloat16)
    return lax.all_to_all(result, "az", split_axis=1, concat_axis=2, tiled=True)


CHUNK = 256
MESH = pl.DeviceIdType.MESH
HP = lax.Precision.HIGHEST
NT = (((1,), (1,)), ((), ()))
TN = (((0,), (0,)), ((), ()))


def host_table(planes):
    row_index = np.arange(planes, dtype=np.int32)
    phase = (row_index[:, None] * (row_index // 2)[None, :]) % planes
    angle = phase.astype(np.float32) * np.float32(2.0 * math.pi / planes)
    even = (row_index % 2 == 0)[None, :]
    table = np.float32(math.sqrt(2.0 / planes)) * np.where(even, np.cos(angle), -np.sin(angle))
    return table.astype(np.float32).astype(ml_dtypes.bfloat16)


def iota(shape, dim):
    return lax.broadcasted_iota(jnp.int32, shape, dim)


def dot_f32(a, b, dims):
    return lax.dot_general(a, b, dims, precision=HP, preferred_element_type=jnp.float32)


def dot_bf16(a, b, dims=(((1,), (0,)), ((), ()))):
    return lax.dot_general(a, b, dims, preferred_element_type=jnp.float32)


def geometry_row(geo, cells, nodes):
    rows = geo.shape[0]
    spread = (iota((cells, nodes), 1) % cells == iota((cells, nodes), 0)).astype(jnp.float32)
    wide = dot_f32(geo, spread, (((1,), (0,)), ((), ())))
    own = iota((rows, nodes), 1) // cells == iota((rows, nodes), 0)
    return jnp.sum(jnp.where(own, wide, 0.0), axis=0, keepdims=True)


def slope_matrices(der, metric_r, metric_z, rows, cells, edge):
    elem = der.shape[1]
    nodes = rows * cells
    left, right = iota((nodes, nodes), 0), iota((nodes, nodes), 1)
    by_row = (iota((nodes, elem), 0) // cells == iota((nodes, elem), 1)).astype(jnp.float32)
    by_axial = (iota((nodes, elem), 0) % elem == iota((nodes, elem), 1)).astype(jnp.float32)
    radial = dot_f32(dot_f32(by_row, der[0], NT), by_row, NT)
    radial = jnp.where(left % cells == right % cells, radial, 0.0) * metric_r
    axial = dot_f32(dot_f32(by_axial, der[1], NT), by_axial, NT)
    axial = jnp.where(left // elem == right // elem, axial, 0.0) * metric_z
    following = pltpu.roll(axial, nodes - 1, 1)
    previous = pltpu.roll(axial, 1, 1)
    cell = right % cells
    last = (cell % elem == elem - 1) & (cell != cells - 1)
    first = (cell % elem == 0) & (cell != 0)
    mean = jnp.where(last, 0.5 * (axial + following), axial)
    mean = jnp.where(first, 0.5 * (axial + previous), mean)
    mean = jnp.where(cell == edge, 0.5 * axial, mean)
    return radial, mean


def fused_kernel(
    n,
    slots,
    vm,
    geo,
    der,
    loads,
    owner,
    tile,
    sa,
    sm,
    table,
    table_t,
    out,
    recv,
    rhs,
    vel,
    swirl,
    radial,
    axial,
    forcing,
    total,
    res,
    tab_v,
    tabt_v,
    sa_v,
    scaled,
    gmat,
    load_rows,
    ids_send,
    ids_recv,
    pick_send,
    pick_recv,
    face_send,
    face_recv,
    f_send,
    f_recv,
    b_send,
    b_recv,
    small_send,
    small_recv,
    x_send,
    x_recv,
    local_sem,
):
    me = lax.axis_index("az")
    mer = lax.axis_index("mer")
    local = vm.shape[1]
    planes = table.shape[0]
    rows, cells = geo.shape[1], geo.shape[2]
    nodes = rows * cells
    jobs = sm.shape[2]
    steps = planes // CHUNK
    bf16 = jnp.bfloat16

    loading = [
        pltpu.make_async_copy(table, tab_v, local_sem.at[0]),
        pltpu.make_async_copy(table_t, tabt_v, local_sem.at[1]),
        pltpu.make_async_copy(sa.at[0, 0], sa_v, local_sem.at[2]),
    ]

    barrier = pltpu.get_barrier_semaphore()

    def greet(o, carry):
        pl.semaphore_signal(
            barrier, inc=1, device_id=(lax.rem(me + o, n), mer), device_id_type=MESH
        )
        return carry

    lax.fori_loop(1, n, greet, 0)
    pl.semaphore_signal(barrier, inc=1, device_id=(me, 1 - mer), device_id_type=MESH)

    row8 = iota((8, 128), 0) % jobs
    codes = jnp.zeros((8, 128), jnp.int32)
    tiles_per_blade = loads.shape[3] // 128
    for j in range(jobs):
        t = tile[0, 0, j]
        code = owner[t // tiles_per_blade] * tiles_per_blade + lax.rem(t, tiles_per_blade)
        codes = jnp.where(row8 == j, code, codes)
    ids_send[...] = codes
    ids_recv[pl.ds(pl.multiple_of(me * 8, 8), 8), :] = codes

    pl.semaphore_wait(barrier, n)

    def send_ids(o, carry):
        peer = lax.rem(me + o, n)
        pltpu.make_async_remote_copy(
            src_ref=ids_send,
            dst_ref=ids_recv.at[pl.ds(pl.multiple_of(me * 8, 8), 8), :],
            send_sem=small_send.at[0],
            recv_sem=small_recv.at[0],
            device_id=(peer, mer),
            device_id_type=MESH,
        ).start()
        return carry

    lax.fori_loop(1, n, send_ids, 0)

    def send_forward(c):
        def body(o, carry):
            peer = lax.rem(me + o, n)
            pltpu.make_async_remote_copy(
                src_ref=vm.at[c, :, pl.ds(pl.multiple_of(peer * nodes, nodes), nodes)],
                dst_ref=recv.at[c, pl.ds(pl.multiple_of(me * local, local), local), :],
                send_sem=f_send.at[c],
                recv_sem=f_recv.at[c],
                device_id=(peer, mer),
                device_id_type=MESH,
            ).start()
            return carry

        lax.fori_loop(1, n, body, 0)
        pltpu.make_async_copy(
            vm.at[c, :, pl.ds(pl.multiple_of(me * nodes, nodes), nodes)],
            recv.at[c, pl.ds(pl.multiple_of(me * local, local), local), :],
            f_recv.at[c],
        ).start()

    send_forward(0)
    send_forward(1)
    for copy in loading:
        copy.start()

    load_rows[...] = jnp.zeros(load_rows.shape, jnp.float32)
    for s in range(slots):
        load_rows[3 * s : 3 * s + 3, :] = loads[0, s].astype(jnp.float32)

    pltpu.make_async_copy(
        ids_recv.at[pl.ds(0, (n - 1) * 8), :],
        ids_recv.at[pl.ds(0, (n - 1) * 8), :],
        small_recv.at[0],
    ).wait()
    asked = ids_recv[...].reshape(n, 8, 128)
    asked = jnp.concatenate([asked, asked], axis=1).reshape(n * 16, 128)
    part = (iota((n * 16, 128), 0) % 16) // jobs
    slot = asked // tiles_per_blade - me * slots
    wanted = slot * 3 + part
    held = (slot >= 0) & (slot < slots) & (part < 3)
    chosen = jnp.where(held & (iota((n * 16, 128), 1) == wanted), 1.0, 0.0)
    every = dot_bf16(chosen[:, :16].astype(bf16), load_rows[...].astype(bf16))
    tile_of = lax.rem(asked, tiles_per_blade)
    picks = jnp.zeros((n * 16, 128), jnp.float32)
    for t in range(tiles_per_blade):
        picks = picks + jnp.where(tile_of == t, every[:, t * 128 : (t + 1) * 128], 0.0)
    pick_send[...] = picks.astype(bf16)
    pick_recv[pl.ds(pl.multiple_of(me * 16, 16), 16), :] = pick_send[
        pl.ds(pl.multiple_of(me * 16, 16), 16), :
    ]

    def send_picks(o, carry):
        peer = lax.rem(me + o, n)
        pltpu.make_async_remote_copy(
            src_ref=pick_send.at[pl.ds(pl.multiple_of(peer * 16, 16), 16), :],
            dst_ref=pick_recv.at[pl.ds(pl.multiple_of(me * 16, 16), 16), :],
            send_sem=small_send.at[1],
            recv_sem=small_recv.at[1],
            device_id=(peer, mer),
            device_id_type=MESH,
        ).start()
        return carry

    lax.fori_loop(1, n, send_picks, 0)
    send_forward(2)

    edge = (1 - mer) * (cells - 1)
    q = geometry_row(geo[0], cells, nodes)
    grad_r, grad_z = slope_matrices(
        der,
        geometry_row(geo[1], cells, nodes),
        geometry_row(geo[2], cells, nodes),
        rows,
        cells,
        edge,
    )
    for side, grad in ((0, grad_r), (1, grad_z)):
        high = grad.astype(bf16)
        low = (grad - high.astype(jnp.float32)).astype(bf16)
        at = slice(side * nodes, (side + 1) * nodes)
        gmat[0:nodes, at] = high
        gmat[nodes : 2 * nodes, at] = high
        gmat[2 * nodes : 3 * nodes, at] = low
    lane = iota((rows, nodes), 1)
    on_edge = (lane // cells == iota((rows, nodes), 0)) & (lane % cells == edge)
    take_edge = jnp.where(on_edge, 2.0, 0.0).astype(bf16)
    put_edge = jnp.where(on_edge, 0.5, 0.0).astype(bf16)

    loading[0].wait()

    def to_planes(c):
        pltpu.make_async_copy(recv.at[c], recv.at[c], f_recv.at[c]).wait()
        modes = recv[c]
        wide = modes.astype(jnp.float32)
        index = iota((planes, nodes), 0)
        wave = (index // 2).astype(jnp.float32) * (2.0 * math.pi / planes)
        after = pltpu.roll(wide, planes - 1, 0)
        before = pltpu.roll(wide, 1, 0)
        slope = jnp.where(index % 2 == 0, -wave * after, wave * before)
        rhs[:, 0:nodes] = modes
        rhs[:, nodes : 2 * nodes] = slope.astype(bf16)

        def body(s, carry):
            at = pl.ds(pl.multiple_of(s * CHUNK, CHUNK), CHUNK)
            both = dot_bf16(tab_v[at, :], rhs[...])
            u = both[:, 0:nodes]
            vel[c, at, :] = u
            swirl[c, at, :] = both[:, nodes : 2 * nodes]
            high = u.astype(bf16)
            low = (u - high.astype(jnp.float32)).astype(bf16)
            slopes = dot_bf16(jnp.concatenate([high, low, high], axis=1), gmat[...])
            radial[c, at, :] = slopes[:, 0:nodes]
            sz = slopes[:, nodes : 2 * nodes]
            axial[c, at, :] = sz
            face_send[c, :, at] = dot_bf16(take_edge, sz.astype(bf16), NT)
            return carry

        lax.fori_loop(0, steps, body, 0)
        copy = pltpu.make_async_remote_copy(
            src_ref=face_send.at[c],
            dst_ref=face_recv.at[c],
            send_sem=x_send.at[c],
            recv_sem=x_recv.at[c],
            device_id=(me, 1 - mer),
            device_id_type=MESH,
        )
        copy.start()
        return copy

    faces = [to_planes(0)]

    pltpu.make_async_copy(
        pick_recv.at[pl.ds(0, (n - 1) * 16), :],
        pick_recv.at[pl.ds(0, (n - 1) * 16), :],
        small_recv.at[1],
    ).wait()
    picked = jnp.sum(pick_recv[...].astype(jnp.float32).reshape(n, 16, 128), axis=0).astype(bf16)
    unit = (iota((128, 128), 0) == iota((128, 128), 1)).astype(jnp.float32).astype(bf16)
    columns = dot_bf16(unit, picked, NT)
    for j in range(jobs):
        weight = sm[0, 0, j].astype(jnp.float32)
        for i in range(3):
            column = columns[:, i * jobs + j : i * jobs + j + 1]
            scaled[j * 128 : (j + 1) * 128, i * nodes : (i + 1) * nodes] = (
                column * weight
            ).astype(bf16)
    loading[2].wait()

    def force(s, carry):
        at = pl.ds(pl.multiple_of(s * CHUNK, CHUNK), CHUNK)
        lhs = sa_v[:, :, at].reshape(jobs * 128, CHUNK)
        forcing[at, :] = dot_bf16(lhs, scaled[...], TN)
        return carry

    lax.fori_loop(0, steps, force, 0)

    faces.append(to_planes(1))
    faces.append(to_planes(2))
    loading[1].wait()

    def to_modes(i):
        faces[i].wait()

        def term(s, carry):
            at = pl.ds(pl.multiple_of(s * CHUNK, CHUNK), CHUNK)
            ur, ut, uz = vel[0, at, :], vel[1, at, :], vel[2, at, :]
            other = dot_bf16(face_recv[i, :, at].astype(bf16), put_edge, TN)
            slope_z = axial[i, at, :] + other
            qt = q * ut
            value = ur * radial[i, at, :] + uz * slope_z + qt * swirl[i, at, :]
            if i == 0:
                value = value - qt * ut
            if i == 1:
                value = value + qt * ur
            total[at, :] = (value + forcing[at, i * nodes : (i + 1) * nodes]).astype(bf16)
            return carry

        lax.fori_loop(0, steps, term, 0)

        def back(s, carry):
            at = pl.ds(pl.multiple_of(s * CHUNK, CHUNK), CHUNK)
            res[i, at, :] = dot_bf16(tabt_v[at, :], total[...]).astype(bf16)
            return carry

        lax.fori_loop(0, steps, back, 0)

        def send(o, carry):
            peer = lax.rem(me + o, n)
            pltpu.make_async_remote_copy(
                src_ref=res.at[i, pl.ds(pl.multiple_of(peer * local, local), local), :],
                dst_ref=out.at[i, :, pl.ds(pl.multiple_of(me * nodes, nodes), nodes)],
                send_sem=b_send.at[i],
                recv_sem=b_recv.at[i],
                device_id=(peer, mer),
                device_id_type=MESH,
            ).start()
            return carry

        lax.fori_loop(1, n, send, 0)
        pltpu.make_async_copy(
            res.at[i, pl.ds(pl.multiple_of(me * local, local), local), :],
            out.at[i, :, pl.ds(pl.multiple_of(me * nodes, nodes), nodes)],
            b_recv.at[i],
        ).start()

    for i in range(3):
        to_modes(i)

    sent = recv.at[0, pl.ds(0, (n - 1) * local), :]
    for c in range(3):
        pltpu.make_async_copy(sent, sent, f_send.at[c]).wait()
        pltpu.make_async_copy(sent, sent, b_send.at[c]).wait()
    sent = ids_recv.at[pl.ds(0, (n - 1) * 8), :]
    pltpu.make_async_copy(sent, sent, small_send.at[0]).wait()
    sent = pick_recv.at[pl.ds(0, (n - 1) * 16), :]
    pltpu.make_async_copy(sent, sent, small_send.at[1]).wait()
    for c in range(3):
        pltpu.make_async_copy(out.at[c], out.at[c], b_recv.at[c]).wait()


def on_device_fused(
    velocity_modes,
    geometry,
    derivative,
    blade_load,
    blade_owner,
    spread_tile,
    spread_azimuth,
    spread_meridional,
):
    n = lax.axis_size("az")
    local = velocity_modes.shape[1]
    planes = n * local
    rows, cells = geometry.shape[1], geometry.shape[2]
    nodes = rows * cells
    jobs = spread_tile.shape[2]
    slots = blade_load.shape[1]
    if local % 16 or lax.axis_size("mer") != 2 or 3 * slots > 16 or jobs != 4:
        return on_device(
            velocity_modes,
            geometry,
            derivative,
            blade_load,
            blade_owner,
            spread_tile,
            spread_azimuth,
            spread_meridional,
        )
    table = host_table(planes)
    bf16, f32 = jnp.bfloat16, jnp.float32
    vmem = pl.BlockSpec(memory_space=pltpu.VMEM)
    smem = pl.BlockSpec(memory_space=pltpu.SMEM)
    hbm = pl.BlockSpec(memory_space=pl.ANY)
    dma = pltpu.SemaphoreType.DMA
    return pl.pallas_call(
        functools.partial(fused_kernel, n, slots),
        out_shape=jax.ShapeDtypeStruct(velocity_modes.shape, bf16),
        in_specs=[hbm, vmem, vmem, vmem, smem, smem, hbm, vmem, hbm, hbm],
        out_specs=hbm,
        scratch_shapes=[
            pltpu.VMEM((3, planes, nodes), bf16),
            pltpu.VMEM((planes, 2 * nodes), bf16),
            pltpu.VMEM((3, planes, nodes), f32),
            pltpu.VMEM((3, planes, nodes), f32),
            pltpu.VMEM((3, planes, nodes), f32),
            pltpu.VMEM((3, planes, nodes), f32),
            pltpu.VMEM((planes, 3 * nodes), f32),
            pltpu.VMEM((planes, nodes), bf16),
            pltpu.VMEM((3, planes, nodes), bf16),
            pltpu.VMEM((planes, planes), bf16),
            pltpu.VMEM((planes, planes), bf16),
            pltpu.VMEM((jobs, TILE, planes), bf16),
            pltpu.VMEM((jobs * TILE, 3 * nodes), bf16),
            pltpu.VMEM((3 * nodes, 2 * nodes), bf16),
            pltpu.VMEM((16, blade_load.shape[3]), f32),
            pltpu.VMEM((8, 128), jnp.int32),
            pltpu.VMEM((n * 8, 128), jnp.int32),
            pltpu.VMEM((n * 16, 128), bf16),
            pltpu.VMEM((n * 16, 128), bf16),
            pltpu.VMEM((3, rows, planes), f32),
            pltpu.VMEM((3, rows, planes), f32),
            dma((3,)),
            dma((3,)),
            dma((3,)),
            dma((3,)),
            dma((2,)),
            dma((2,)),
            dma((3,)),
            dma((3,)),
            dma((3,)),
        ],
        compiler_params=pltpu.CompilerParams(
            collective_id=0, has_side_effects=True, vmem_limit_bytes=48 * 1024 * 1024
        ),
    )(
        velocity_modes,
        geometry,
        derivative,
        blade_load,
        blade_owner,
        spread_tile,
        spread_azimuth,
        spread_meridional,
        jnp.asarray(table),
        jnp.asarray(np.ascontiguousarray(table.T)),
    )


def solution(mesh):
    in_specs = (
        P(None, "az", "mer"),
        P(None, "az", "mer"),
        P(),
        P("az", None, None, None),
        P(),
        P("mer", "az", None),
        P("mer", "az", None, None, None),
        P("mer", "az", None, None, None),
    )
    out_specs = P(None, "az", "mer")
    return jax.shard_map(
        on_device_fused, mesh=mesh, in_specs=in_specs, out_specs=out_specs, check_vma=False
    )
```

```python
import functools
import math

import jax
import jax.numpy as jnp
import ml_dtypes
import numpy as np
from jax import lax
from jax.experimental import pallas as pl
from jax.experimental.pallas import tpu as pltpu
from jax.sharding import PartitionSpec as P

PLANES = 1024
TILE = 128


def extended(shard, sides, width):
    for axis, dim in sides:
        count, length = (lax.axis_size(axis), shard.shape[dim])
        up = [(i, (i + 1) % count) for i in range(count - 1)]
        down = [(j, i) for i, j in up]
        last = lax.slice_in_dim(shard, length - width, length, axis=dim)
        leading = lax.slice_in_dim(shard, 0, width, axis=dim)
        before = lax.ppermute(last, axis, up)
        after = lax.ppermute(leading, axis, down)
        shard = jnp.concatenate([before, shard, after], axis=dim)
    return shard


def make_table(planes):
    row_index = jnp.arange(planes, dtype=jnp.int32)
    wave_index = row_index // 2
    phase_index = row_index[:, None] * wave_index[None, :] % planes
    angle_rad = phase_index.astype(jnp.float32) * (2.0 * math.pi / planes)
    even_rows = (row_index % 2 == 0)[None, :]
    dft_table = math.sqrt(2.0 / planes) * jnp.where(
        even_rows, jnp.cos(angle_rad), -jnp.sin(angle_rad)
    )
    return dft_table.astype(jnp.bfloat16)


def slope_of(mode_block, first_pair, planes):
    shape_all = mode_block.shape
    mode_pairs = mode_block.reshape(shape_all[0], shape_all[1] // 2, 2, shape_all[2]).astype(
        jnp.float32
    )
    wave_number = (first_pair + jnp.arange(shape_all[1] // 2, dtype=jnp.int32)).astype(
        jnp.float32
    ) * (2.0 * math.pi / planes)
    wave_number = wave_number[None, :, None]
    result = jnp.stack(
        [-wave_number * mode_pairs[:, :, 1], wave_number * mode_pairs[:, :, 0]], axis=2
    )
    return result.reshape(shape_all).astype(jnp.bfloat16)


def inverse_of(dft_table, mode_block):
    return jnp.einsum("pj,cjn->cpn", dft_table, mode_block, preferred_element_type=jnp.float32)


def slopes_of(velocity, geometry, derivative):
    hp = lax.Precision.HIGHEST
    shape_all = velocity.shape
    elem_size = derivative.shape[1]
    elements = shape_all[3] // elem_size
    radial_slope = geometry[1] * jnp.einsum("rs,cpsz->cprz", derivative[0], velocity, precision=hp)
    blocks = velocity.reshape(shape_all[0], shape_all[1], shape_all[2], elements, elem_size)
    raw_slope = jnp.einsum("at,cpret->cprea", derivative[1], blocks, precision=hp)
    axial_slope = raw_slope * geometry[2].reshape(shape_all[2], elements, elem_size)
    first_face = axial_slope[..., 0]
    last_face = axial_slope[..., elem_size - 1]
    face_mean = 0.5 * (last_face[..., :-1] + first_face[..., 1:])
    new_first = first_face.at[..., 1:].set(face_mean)
    new_last = last_face.at[..., :-1].set(face_mean)
    return (radial_slope, axial_slope, first_face, last_face, new_first, new_last)


def advect(velocity, radial_slope, axial_slope, swirl_slope, inverse_radius):
    radial_vel = velocity[0]
    swirl_vel = velocity[1]
    axial_vel = velocity[2]
    advection = (
        radial_vel[None] * radial_slope
        + axial_vel[None] * axial_slope
        + (inverse_radius * swirl_vel)[None] * swirl_slope
    )
    advection = advection.at[0].add(-(inverse_radius * swirl_vel * swirl_vel))
    advection = advection.at[1].add(inverse_radius * radial_vel * swirl_vel)
    return advection


def forcing_of(all_loads, tile_ids, spread_az, spread_mer, tile_size):
    blades = all_loads.shape[0]
    tiles_count = all_loads.shape[2] // tile_size
    tile_loads = (
        all_loads.reshape(blades, 3, tiles_count, tile_size)
        .transpose(0, 2, 1, 3)
        .reshape(blades * tiles_count, 3, tile_size)
    )
    picked = jnp.take(tile_loads, tile_ids, axis=0)
    scaled = (
        picked.astype(jnp.float32)[:, :, :, None] * spread_mer.astype(jnp.float32)[:, None, :, :]
    ).astype(jnp.bfloat16)
    return jnp.einsum("jmp,jcmn->cpn", spread_az, scaled, preferred_element_type=jnp.float32)


def on_device(
    velocity_modes,
    geometry,
    derivative,
    blade_load,
    blade_owner,
    spread_tile,
    spread_azimuth,
    spread_meridional,
):
    planes = PLANES
    dft_table = make_table(planes)
    local_modes = velocity_modes.shape[1]
    block_cells = geometry.shape[1] * geometry.shape[2]
    first_pair = lax.axis_index("az") * (local_modes // 2)
    slope_local = slope_of(velocity_modes, first_pair, planes)
    velocity = inverse_of(
        dft_table, lax.all_to_all(velocity_modes, "az", split_axis=2, concat_axis=1, tiled=True)
    )
    swirl_slope = inverse_of(
        dft_table, lax.all_to_all(slope_local, "az", split_axis=2, concat_axis=1, tiled=True)
    )
    rows = geometry.shape[1]
    cells = geometry.shape[2]
    velocity = velocity.reshape(3, planes, rows, cells)
    swirl_slope = swirl_slope.reshape(3, planes, rows, cells)
    radial_slope, axial_slope, first_face, last_face, new_first, new_last = slopes_of(
        velocity, geometry, derivative
    )
    edge_values = jnp.stack([first_face[..., 0], last_face[..., -1]], axis=-1)
    padded = extended(edge_values.astype(jnp.bfloat16), (("mer", 3),), 1).astype(edge_values.dtype)
    mer_index = lax.axis_index("mer")
    mer_count = lax.axis_size("mer")
    left_value = jnp.where(
        mer_index > 0, 0.5 * (padded[..., 0] + first_face[..., 0]), first_face[..., 0]
    )
    right_value = jnp.where(
        mer_index < mer_count - 1, 0.5 * (last_face[..., -1] + padded[..., 3]), last_face[..., -1]
    )
    new_first = new_first.at[..., 0].set(left_value)
    new_last = new_last.at[..., -1].set(right_value)
    elem_size = derivative.shape[1]
    axial_slope = axial_slope.at[..., 0].set(new_first).at[..., elem_size - 1].set(new_last)
    axial_slope = axial_slope.reshape(3, planes, rows, cells)
    advection = advect(velocity, radial_slope, axial_slope, swirl_slope, geometry[0])
    local_slots = blade_load[0]
    every_slot = lax.all_gather(blade_load, "az", axis=0, tiled=True)
    all_loads = every_slot.reshape(-1, 3, local_slots.shape[2])[blade_owner]
    forcing = forcing_of(
        all_loads, spread_tile[0, 0], spread_azimuth[0, 0], spread_meridional[0, 0], TILE
    )
    total_term = (advection.reshape(3, planes, block_cells) + forcing).astype(jnp.bfloat16)
    result = jnp.einsum(
        "pj,cpn->cjn", dft_table, total_term, preferred_element_type=jnp.float32
    ).astype(jnp.bfloat16)
    return lax.all_to_all(result, "az", split_axis=1, concat_axis=2, tiled=True)


CHUNK = 256
MESH = pl.DeviceIdType.MESH
HP = lax.Precision.HIGHEST
NT = (((1,), (1,)), ((), ()))
TN = (((0,), (0,)), ((), ()))


def host_table(planes):
    row_index = np.arange(planes, dtype=np.int32)
    phase = (row_index[:, None] * (row_index // 2)[None, :]) % planes
    angle = phase.astype(np.float32) * np.float32(2.0 * math.pi / planes)
    even = (row_index % 2 == 0)[None, :]
    table = np.float32(math.sqrt(2.0 / planes)) * np.where(even, np.cos(angle), -np.sin(angle))
    return table.astype(np.float32).astype(ml_dtypes.bfloat16)


def iota(shape, dim):
    return lax.broadcasted_iota(jnp.int32, shape, dim)


def dot_f32(a, b, dims):
    return lax.dot_general(a, b, dims, precision=HP, preferred_element_type=jnp.float32)


def dot_bf16(a, b, dims=(((1,), (0,)), ((), ()))):
    return lax.dot_general(a, b, dims, preferred_element_type=jnp.float32)


def geometry_row(geo, cells, nodes):
    rows = geo.shape[0]
    spread = (iota((cells, nodes), 1) % cells == iota((cells, nodes), 0)).astype(jnp.float32)
    wide = dot_f32(geo, spread, (((1,), (0,)), ((), ())))
    own = iota((rows, nodes), 1) // cells == iota((rows, nodes), 0)
    return jnp.sum(jnp.where(own, wide, 0.0), axis=0, keepdims=True)


def slope_matrices(der, metric_r, metric_z, rows, cells, edge):
    elem = der.shape[1]
    nodes = rows * cells
    left, right = iota((nodes, nodes), 0), iota((nodes, nodes), 1)
    by_row = (iota((nodes, elem), 0) // cells == iota((nodes, elem), 1)).astype(jnp.float32)
    by_axial = (iota((nodes, elem), 0) % elem == iota((nodes, elem), 1)).astype(jnp.float32)
    radial = dot_f32(dot_f32(by_row, der[0], NT), by_row, NT)
    radial = jnp.where(left % cells == right % cells, radial, 0.0) * metric_r
    axial = dot_f32(dot_f32(by_axial, der[1], NT), by_axial, NT)
    axial = jnp.where(left // elem == right // elem, axial, 0.0) * metric_z
    following = pltpu.roll(axial, nodes - 1, 1)
    previous = pltpu.roll(axial, 1, 1)
    cell = right % cells
    last = (cell % elem == elem - 1) & (cell != cells - 1)
    first = (cell % elem == 0) & (cell != 0)
    mean = jnp.where(last, 0.5 * (axial + following), axial)
    mean = jnp.where(first, 0.5 * (axial + previous), mean)
    mean = jnp.where(cell == edge, 0.5 * axial, mean)
    return radial, mean


def fused_kernel(
    n,
    slots,
    vm,
    geo_in,
    der_in,
    loads,
    owner,
    tile,
    sa,
    sm_in,
    table,
    table_t,
    out,
    recv,
    rhs,
    vel,
    swirl,
    radial,
    axial,
    forcing,
    total,
    res,
    tab_v,
    tabt_v,
    sa_v,
    sm,
    geo,
    der,
    scaled,
    gmat,
    load_rows,
    ids_send,
    ids_recv,
    pick_send,
    pick_recv,
    face_send,
    face_recv,
    f_send,
    f_recv,
    b_send,
    b_recv,
    small_send,
    small_recv,
    x_send,
    x_recv,
    local_sem,
):
    me = lax.axis_index("az")
    mer = lax.axis_index("mer")
    local = vm.shape[1]
    planes = table.shape[0]
    rows, cells = geo.shape[1], geo.shape[2]
    nodes = rows * cells
    jobs = sm.shape[0]
    steps = planes // CHUNK
    bf16 = jnp.bfloat16

    barrier = pltpu.get_barrier_semaphore()

    def greet(o, carry):
        pl.semaphore_signal(
            barrier, inc=1, device_id=(lax.rem(me + o, n), mer), device_id_type=MESH
        )
        return carry

    lax.fori_loop(1, n, greet, 0)
    pl.semaphore_signal(barrier, inc=1, device_id=(me, 1 - mer), device_id_type=MESH)

    loading = [
        pltpu.make_async_copy(geo_in, geo, local_sem.at[0]),
        pltpu.make_async_copy(der_in, der, local_sem.at[1]),
        pltpu.make_async_copy(sm_in.at[0, 0], sm, local_sem.at[2]),
        pltpu.make_async_copy(sa.at[0, 0], sa_v, local_sem.at[3]),
        pltpu.make_async_copy(table, tab_v, local_sem.at[4]),
        pltpu.make_async_copy(table_t, tabt_v, local_sem.at[5]),
    ]

    row8 = iota((8, 128), 0) % jobs
    codes = jnp.zeros((8, 128), jnp.int32)
    tiles_per_blade = loads.shape[3] // 128
    for j in range(jobs):
        t = tile[0, 0, j]
        code = owner[t // tiles_per_blade] * tiles_per_blade + lax.rem(t, tiles_per_blade)
        codes = jnp.where(row8 == j, code, codes)
    ids_send[...] = codes
    ids_recv[pl.ds(pl.multiple_of(me * 8, 8), 8), :] = codes

    pl.semaphore_wait(barrier, n)

    def send_ids(o, carry):
        peer = lax.rem(me + o, n)
        pltpu.make_async_remote_copy(
            src_ref=ids_send,
            dst_ref=ids_recv.at[pl.ds(pl.multiple_of(me * 8, 8), 8), :],
            send_sem=small_send.at[0],
            recv_sem=small_recv.at[0],
            device_id=(peer, mer),
            device_id_type=MESH,
        ).start()
        return carry

    lax.fori_loop(1, n, send_ids, 0)

    def send_forward(c):
        def body(o, carry):
            peer = lax.rem(me + o, n)
            pltpu.make_async_remote_copy(
                src_ref=vm.at[c, :, pl.ds(pl.multiple_of(peer * nodes, nodes), nodes)],
                dst_ref=recv.at[c, pl.ds(pl.multiple_of(me * local, local), local), :],
                send_sem=f_send.at[c],
                recv_sem=f_recv.at[c],
                device_id=(peer, mer),
                device_id_type=MESH,
            ).start()
            return carry

        lax.fori_loop(1, n, body, 0)
        pltpu.make_async_copy(
            vm.at[c, :, pl.ds(pl.multiple_of(me * nodes, nodes), nodes)],
            recv.at[c, pl.ds(pl.multiple_of(me * local, local), local), :],
            f_recv.at[c],
        ).start()

    send_forward(0)
    for copy in loading:
        copy.start()

    load_rows[...] = jnp.zeros(load_rows.shape, jnp.float32)
    for s in range(slots):
        load_rows[3 * s : 3 * s + 3, :] = loads[0, s].astype(jnp.float32)

    pltpu.make_async_copy(
        ids_recv.at[pl.ds(0, (n - 1) * 8), :],
        ids_recv.at[pl.ds(0, (n - 1) * 8), :],
        small_recv.at[0],
    ).wait()
    asked = ids_recv[...].reshape(n, 8, 128)
    asked = jnp.concatenate([asked, asked], axis=1).reshape(n * 16, 128)
    part = (iota((n * 16, 128), 0) % 16) // jobs
    slot = asked // tiles_per_blade - me * slots
    wanted = slot * 3 + part
    held = (slot >= 0) & (slot < slots) & (part < 3)
    chosen = jnp.where(held & (iota((n * 16, 128), 1) == wanted), 1.0, 0.0)
    every = dot_bf16(chosen[:, :16].astype(bf16), load_rows[...].astype(bf16))
    tile_of = lax.rem(asked, tiles_per_blade)
    picks = jnp.zeros((n * 16, 128), jnp.float32)
    for t in range(tiles_per_blade):
        picks = picks + jnp.where(tile_of == t, every[:, t * 128 : (t + 1) * 128], 0.0)
    pick_send[...] = picks.astype(bf16)
    pick_recv[pl.ds(pl.multiple_of(me * 16, 16), 16), :] = pick_send[
        pl.ds(pl.multiple_of(me * 16, 16), 16), :
    ]

    def send_picks(o, carry):
        peer = lax.rem(me + o, n)
        pltpu.make_async_remote_copy(
            src_ref=pick_send.at[pl.ds(pl.multiple_of(peer * 16, 16), 16), :],
            dst_ref=pick_recv.at[pl.ds(pl.multiple_of(me * 16, 16), 16), :],
            send_sem=small_send.at[1],
            recv_sem=small_recv.at[1],
            device_id=(peer, mer),
            device_id_type=MESH,
        ).start()
        return carry

    lax.fori_loop(1, n, send_picks, 0)
    send_forward(1)
    send_forward(2)

    loading[0].wait()
    loading[1].wait()
    edge = (1 - mer) * (cells - 1)
    q = geometry_row(geo[0], cells, nodes)
    grad_r, grad_z = slope_matrices(
        der,
        geometry_row(geo[1], cells, nodes),
        geometry_row(geo[2], cells, nodes),
        rows,
        cells,
        edge,
    )
    for side, grad in ((0, grad_r), (1, grad_z)):
        high = grad.astype(bf16)
        low = (grad - high.astype(jnp.float32)).astype(bf16)
        at = slice(side * nodes, (side + 1) * nodes)
        gmat[0:nodes, at] = high
        gmat[nodes : 2 * nodes, at] = high
        gmat[2 * nodes : 3 * nodes, at] = low
    lane = iota((rows, nodes), 1)
    on_edge = (lane // cells == iota((rows, nodes), 0)) & (lane % cells == edge)
    take_edge = jnp.where(on_edge, 2.0, 0.0).astype(bf16)
    put_edge = jnp.where(on_edge, 0.5, 0.0).astype(bf16)

    def over_planes(body, unroll=False):
        def step(s, carry):
            body(pl.ds(pl.multiple_of(s * CHUNK, CHUNK), CHUNK))
            return carry

        lax.fori_loop(0, steps, step, 0, unroll=unroll)

    def arrived(c):
        pltpu.make_async_copy(recv.at[c], recv.at[c], f_recv.at[c]).wait()

    def slope_modes(c):
        wide = recv[c].astype(jnp.float32)
        index = iota((planes, nodes), 0)
        wave = (index // 2).astype(jnp.float32) * (2.0 * math.pi / planes)
        after = pltpu.roll(wide, planes - 1, 0)
        before = pltpu.roll(wide, 1, 0)
        rhs[:, nodes : 2 * nodes] = jnp.where(
            index % 2 == 0, -wave * after, wave * before
        ).astype(bf16)

    def slopes_at(c, at, u):
        high = u.astype(bf16)
        low = (u - high.astype(jnp.float32)).astype(bf16)
        slopes = dot_bf16(jnp.concatenate([high, low, high], axis=1), gmat[...])
        radial[c, at, :] = slopes[:, 0:nodes]
        sz = slopes[:, nodes : 2 * nodes]
        axial[c, at, :] = sz
        face_send[c, :, at] = dot_bf16(take_edge, sz.astype(bf16), NT)

    def face_copy(c):
        return pltpu.make_async_remote_copy(
            src_ref=face_send.at[c],
            dst_ref=face_recv.at[c],
            send_sem=x_send.at[c],
            recv_sem=x_recv.at[c],
            device_id=(me, 1 - mer),
            device_id_type=MESH,
        )

    def to_planes(c):
        arrived(c)
        slope_modes(c)
        rhs[:, 0:nodes] = recv[c]

        def body(at):
            both = dot_bf16(tab_v[at, :], rhs[...])
            u = both[:, 0:nodes]
            vel[c, at, :] = u
            swirl[c, at, :] = both[:, nodes : 2 * nodes]
            slopes_at(c, at, u)

        over_planes(body)
        face_copy(c).start()

    loading[2].wait()
    pltpu.make_async_copy(
        pick_recv.at[pl.ds(0, (n - 1) * 16), :],
        pick_recv.at[pl.ds(0, (n - 1) * 16), :],
        small_recv.at[1],
    ).wait()
    picked = jnp.sum(pick_recv[...].astype(jnp.float32).reshape(n, 16, 128), axis=0).astype(bf16)
    unit = (iota((128, 128), 0) == iota((128, 128), 1)).astype(jnp.float32).astype(bf16)
    columns = dot_bf16(unit, picked, NT)
    for j in range(jobs):
        weight = sm[j].astype(jnp.float32)
        for i in range(3):
            column = columns[:, i * jobs + j : i * jobs + j + 1]
            scaled[j * 128 : (j + 1) * 128, i * nodes : (i + 1) * nodes] = (
                column * weight
            ).astype(bf16)
    loading[3].wait()

    def force(at):
        lhs = sa_v[:, :, at].reshape(jobs * 128, CHUNK)
        forcing[at, :] = dot_bf16(lhs, scaled[...], TN)

    over_planes(force)
    loading[4].wait()
    to_planes(0)
    to_planes(1)

    for i in range(2):
        face_copy(i).wait()

    def partial(at):
        ur, ut = vel[0, at, :], vel[1, at, :]
        qt = q * ut
        for i in range(2):
            other = dot_bf16(face_recv[i, :, at].astype(bf16), put_edge, TN)
            axial[i, at, :] = axial[i, at, :] + other
            value = ur * radial[i, at, :] + qt * swirl[i, at, :]
            value = value - qt * ut if i == 0 else value + qt * ur
            radial[i, at, :] = value + forcing[at, i * nodes : (i + 1) * nodes]

    over_planes(partial)
    loading[5].wait()

    arrived(2)

    def first_terms(at):
        uz = dot_bf16(tab_v[at, :], recv[2])
        vel[2, at, :] = uz
        for i in range(2):
            total[at, i * nodes : (i + 1) * nodes] = (
                radial[i, at, :] + uz * axial[i, at, :]
            ).astype(bf16)

    over_planes(first_terms, True)

    peers = CHUNK // local
    chunk_of, seat = me // peers, lax.rem(me, peers)

    def to_modes(components):
        count = len(components)
        for k in (2, 3, 1, 0):
            chunk = lax.rem(chunk_of + k, steps)
            at = pl.ds(pl.multiple_of(chunk * CHUNK, CHUNK), CHUNK)
            back = dot_bf16(tabt_v[at, :], total[:, 0 : count * nodes])
            for d, i in enumerate(components):
                res[i, at, :] = back[:, d * nodes : (d + 1) * nodes].astype(bf16)
            for i in components:

                def send(o, carry):
                    peer = chunk * peers + lax.rem(seat + o, peers)
                    pltpu.make_async_remote_copy(
                        src_ref=res.at[i, pl.ds(pl.multiple_of(peer * local, local), local), :],
                        dst_ref=out.at[i, :, pl.ds(pl.multiple_of(me * nodes, nodes), nodes)],
                        send_sem=b_send.at[i],
                        recv_sem=b_recv.at[i],
                        device_id=(peer, mer),
                        device_id_type=MESH,
                    ).start()
                    return carry

                lax.fori_loop(1 if k == 0 else 0, peers, send, 0)
        for i in components:
            pltpu.make_async_copy(
                res.at[i, pl.ds(pl.multiple_of(me * local, local), local), :],
                out.at[i, :, pl.ds(pl.multiple_of(me * nodes, nodes), nodes)],
                b_recv.at[i],
            ).start()

    to_modes((0, 1))

    slope_modes(2)

    def own_slopes(at):
        swirl[2, at, :] = dot_bf16(tab_v[at, :], rhs[:, nodes : 2 * nodes])
        slopes_at(2, at, vel[2, at, :])

    over_planes(own_slopes)
    face_copy(2).start()
    face_copy(2).wait()

    def last_term(at):
        other = dot_bf16(face_recv[2, :, at].astype(bf16), put_edge, TN)
        value = vel[0, at, :] * radial[2, at, :] + vel[2, at, :] * (axial[2, at, :] + other)
        value = value + (q * vel[1, at, :]) * swirl[2, at, :]
        total[at, 0:nodes] = (value + forcing[at, 2 * nodes : 3 * nodes]).astype(bf16)

    over_planes(last_term)
    to_modes((2,))

    sent = recv.at[0, pl.ds(0, (n - 1) * local), :]
    for c in range(3):
        pltpu.make_async_copy(sent, sent, f_send.at[c]).wait()
        pltpu.make_async_copy(sent, sent, b_send.at[c]).wait()
    sent = ids_recv.at[pl.ds(0, (n - 1) * 8), :]
    pltpu.make_async_copy(sent, sent, small_send.at[0]).wait()
    sent = pick_recv.at[pl.ds(0, (n - 1) * 16), :]
    pltpu.make_async_copy(sent, sent, small_send.at[1]).wait()
    for c in range(3):
        pltpu.make_async_copy(out.at[c], out.at[c], b_recv.at[c]).wait()


def on_device_fused(
    velocity_modes,
    geometry,
    derivative,
    blade_load,
    blade_owner,
    spread_tile,
    spread_azimuth,
    spread_meridional,
):
    n = lax.axis_size("az")
    local = velocity_modes.shape[1]
    planes = n * local
    rows, cells = geometry.shape[1], geometry.shape[2]
    nodes = rows * cells
    jobs = spread_tile.shape[2]
    slots = blade_load.shape[1]
    if local % 16 or planes != 4 * CHUNK or CHUNK % local or lax.axis_size("mer") != 2 or 3 * slots > 16 or jobs != 4:
        return on_device(
            velocity_modes,
            geometry,
            derivative,
            blade_load,
            blade_owner,
            spread_tile,
            spread_azimuth,
            spread_meridional,
        )
    table = host_table(planes)
    bf16, f32 = jnp.bfloat16, jnp.float32
    vmem = pl.BlockSpec(memory_space=pltpu.VMEM)
    smem = pl.BlockSpec(memory_space=pltpu.SMEM)
    hbm = pl.BlockSpec(memory_space=pl.ANY)
    dma = pltpu.SemaphoreType.DMA
    return pl.pallas_call(
        functools.partial(fused_kernel, n, slots),
        out_shape=jax.ShapeDtypeStruct(velocity_modes.shape, bf16),
        in_specs=[hbm, hbm, hbm, vmem, smem, smem, hbm, hbm, hbm, hbm],
        out_specs=hbm,
        scratch_shapes=[
            pltpu.VMEM((3, planes, nodes), bf16),
            pltpu.VMEM((planes, 2 * nodes), bf16),
            pltpu.VMEM((3, planes, nodes), f32),
            pltpu.VMEM((3, planes, nodes), f32),
            pltpu.VMEM((3, planes, nodes), f32),
            pltpu.VMEM((3, planes, nodes), f32),
            pltpu.VMEM((planes, 3 * nodes), f32),
            pltpu.VMEM((planes, 2 * nodes), bf16),
            pltpu.VMEM((3, planes, nodes), bf16),
            pltpu.VMEM((planes, planes), bf16),
            pltpu.VMEM((planes, planes), bf16),
            pltpu.VMEM((jobs, TILE, planes), bf16),
            pltpu.VMEM((jobs, TILE, nodes), bf16),
            pltpu.VMEM(geometry.shape, f32),
            pltpu.VMEM(derivative.shape, f32),
            pltpu.VMEM((jobs * TILE, 3 * nodes), bf16),
            pltpu.VMEM((3 * nodes, 2 * nodes), bf16),
            pltpu.VMEM((16, blade_load.shape[3]), f32),
            pltpu.VMEM((8, 128), jnp.int32),
            pltpu.VMEM((n * 8, 128), jnp.int32),
            pltpu.VMEM((n * 16, 128), bf16),
            pltpu.VMEM((n * 16, 128), bf16),
            pltpu.VMEM((3, rows, planes), f32),
            pltpu.VMEM((3, rows, planes), f32),
            dma((3,)),
            dma((3,)),
            dma((3,)),
            dma((3,)),
            dma((2,)),
            dma((2,)),
            dma((3,)),
            dma((3,)),
            dma((6,)),
        ],
        compiler_params=pltpu.CompilerParams(
            collective_id=0, has_side_effects=True, vmem_limit_bytes=60 * 1024 * 1024
        ),
    )(
        velocity_modes,
        geometry,
        derivative,
        blade_load,
        blade_owner,
        spread_tile,
        spread_azimuth,
        spread_meridional,
        jnp.asarray(table),
        jnp.asarray(np.ascontiguousarray(table.T)),
    )


def solution(mesh):
    in_specs = (
        P(None, "az", "mer"),
        P(None, "az", "mer"),
        P(),
        P("az", None, None, None),
        P(),
        P("mer", "az", None),
        P("mer", "az", None, None, None),
        P("mer", "az", None, None, None),
    )
    out_specs = P(None, "az", "mer")
    return jax.shard_map(
        on_device_fused, mesh=mesh, in_specs=in_specs, out_specs=out_specs, check_vma=False
    )
```

```python
import functools
import math

import jax
import jax.numpy as jnp
import ml_dtypes
import numpy as np
from jax import lax
from jax.experimental import pallas as pl
from jax.experimental.pallas import tpu as pltpu
from jax.sharding import PartitionSpec as P

PLANES = 1024
TILE = 128


def extended(shard, sides, width):
    for axis, dim in sides:
        count, length = (lax.axis_size(axis), shard.shape[dim])
        up = [(i, (i + 1) % count) for i in range(count - 1)]
        down = [(j, i) for i, j in up]
        last = lax.slice_in_dim(shard, length - width, length, axis=dim)
        leading = lax.slice_in_dim(shard, 0, width, axis=dim)
        before = lax.ppermute(last, axis, up)
        after = lax.ppermute(leading, axis, down)
        shard = jnp.concatenate([before, shard, after], axis=dim)
    return shard


def make_table(planes):
    row_index = jnp.arange(planes, dtype=jnp.int32)
    wave_index = row_index // 2
    phase_index = row_index[:, None] * wave_index[None, :] % planes
    angle_rad = phase_index.astype(jnp.float32) * (2.0 * math.pi / planes)
    even_rows = (row_index % 2 == 0)[None, :]
    dft_table = math.sqrt(2.0 / planes) * jnp.where(
        even_rows, jnp.cos(angle_rad), -jnp.sin(angle_rad)
    )
    return dft_table.astype(jnp.bfloat16)


def slope_of(mode_block, first_pair, planes):
    shape_all = mode_block.shape
    mode_pairs = mode_block.reshape(shape_all[0], shape_all[1] // 2, 2, shape_all[2]).astype(
        jnp.float32
    )
    wave_number = (first_pair + jnp.arange(shape_all[1] // 2, dtype=jnp.int32)).astype(
        jnp.float32
    ) * (2.0 * math.pi / planes)
    wave_number = wave_number[None, :, None]
    result = jnp.stack(
        [-wave_number * mode_pairs[:, :, 1], wave_number * mode_pairs[:, :, 0]], axis=2
    )
    return result.reshape(shape_all).astype(jnp.bfloat16)


def inverse_of(dft_table, mode_block):
    return jnp.einsum("pj,cjn->cpn", dft_table, mode_block, preferred_element_type=jnp.float32)


def slopes_of(velocity, geometry, derivative):
    hp = lax.Precision.HIGHEST
    shape_all = velocity.shape
    elem_size = derivative.shape[1]
    elements = shape_all[3] // elem_size
    radial_slope = geometry[1] * jnp.einsum("rs,cpsz->cprz", derivative[0], velocity, precision=hp)
    blocks = velocity.reshape(shape_all[0], shape_all[1], shape_all[2], elements, elem_size)
    raw_slope = jnp.einsum("at,cpret->cprea", derivative[1], blocks, precision=hp)
    axial_slope = raw_slope * geometry[2].reshape(shape_all[2], elements, elem_size)
    first_face = axial_slope[..., 0]
    last_face = axial_slope[..., elem_size - 1]
    face_mean = 0.5 * (last_face[..., :-1] + first_face[..., 1:])
    new_first = first_face.at[..., 1:].set(face_mean)
    new_last = last_face.at[..., :-1].set(face_mean)
    return (radial_slope, axial_slope, first_face, last_face, new_first, new_last)


def advect(velocity, radial_slope, axial_slope, swirl_slope, inverse_radius):
    radial_vel = velocity[0]
    swirl_vel = velocity[1]
    axial_vel = velocity[2]
    advection = (
        radial_vel[None] * radial_slope
        + axial_vel[None] * axial_slope
        + (inverse_radius * swirl_vel)[None] * swirl_slope
    )
    advection = advection.at[0].add(-(inverse_radius * swirl_vel * swirl_vel))
    advection = advection.at[1].add(inverse_radius * radial_vel * swirl_vel)
    return advection


def forcing_of(all_loads, tile_ids, spread_az, spread_mer, tile_size):
    blades = all_loads.shape[0]
    tiles_count = all_loads.shape[2] // tile_size
    tile_loads = (
        all_loads.reshape(blades, 3, tiles_count, tile_size)
        .transpose(0, 2, 1, 3)
        .reshape(blades * tiles_count, 3, tile_size)
    )
    picked = jnp.take(tile_loads, tile_ids, axis=0)
    scaled = (
        picked.astype(jnp.float32)[:, :, :, None] * spread_mer.astype(jnp.float32)[:, None, :, :]
    ).astype(jnp.bfloat16)
    return jnp.einsum("jmp,jcmn->cpn", spread_az, scaled, preferred_element_type=jnp.float32)


def on_device(
    velocity_modes,
    geometry,
    derivative,
    blade_load,
    blade_owner,
    spread_tile,
    spread_azimuth,
    spread_meridional,
):
    planes = PLANES
    dft_table = make_table(planes)
    local_modes = velocity_modes.shape[1]
    block_cells = geometry.shape[1] * geometry.shape[2]
    first_pair = lax.axis_index("az") * (local_modes // 2)
    slope_local = slope_of(velocity_modes, first_pair, planes)
    velocity = inverse_of(
        dft_table, lax.all_to_all(velocity_modes, "az", split_axis=2, concat_axis=1, tiled=True)
    )
    swirl_slope = inverse_of(
        dft_table, lax.all_to_all(slope_local, "az", split_axis=2, concat_axis=1, tiled=True)
    )
    rows = geometry.shape[1]
    cells = geometry.shape[2]
    velocity = velocity.reshape(3, planes, rows, cells)
    swirl_slope = swirl_slope.reshape(3, planes, rows, cells)
    radial_slope, axial_slope, first_face, last_face, new_first, new_last = slopes_of(
        velocity, geometry, derivative
    )
    edge_values = jnp.stack([first_face[..., 0], last_face[..., -1]], axis=-1)
    padded = extended(edge_values.astype(jnp.bfloat16), (("mer", 3),), 1).astype(edge_values.dtype)
    mer_index = lax.axis_index("mer")
    mer_count = lax.axis_size("mer")
    left_value = jnp.where(
        mer_index > 0, 0.5 * (padded[..., 0] + first_face[..., 0]), first_face[..., 0]
    )
    right_value = jnp.where(
        mer_index < mer_count - 1, 0.5 * (last_face[..., -1] + padded[..., 3]), last_face[..., -1]
    )
    new_first = new_first.at[..., 0].set(left_value)
    new_last = new_last.at[..., -1].set(right_value)
    elem_size = derivative.shape[1]
    axial_slope = axial_slope.at[..., 0].set(new_first).at[..., elem_size - 1].set(new_last)
    axial_slope = axial_slope.reshape(3, planes, rows, cells)
    advection = advect(velocity, radial_slope, axial_slope, swirl_slope, geometry[0])
    local_slots = blade_load[0]
    every_slot = lax.all_gather(blade_load, "az", axis=0, tiled=True)
    all_loads = every_slot.reshape(-1, 3, local_slots.shape[2])[blade_owner]
    forcing = forcing_of(
        all_loads, spread_tile[0, 0], spread_azimuth[0, 0], spread_meridional[0, 0], TILE
    )
    total_term = (advection.reshape(3, planes, block_cells) + forcing).astype(jnp.bfloat16)
    result = jnp.einsum(
        "pj,cpn->cjn", dft_table, total_term, preferred_element_type=jnp.float32
    ).astype(jnp.bfloat16)
    return lax.all_to_all(result, "az", split_axis=1, concat_axis=2, tiled=True)


CHUNK = 256
MESH = pl.DeviceIdType.MESH
HP = lax.Precision.HIGHEST
NT = (((1,), (1,)), ((), ()))
TN = (((0,), (0,)), ((), ()))


def host_table(planes):
    row_index = np.arange(planes, dtype=np.int32)
    phase = (row_index[:, None] * (row_index // 2)[None, :]) % planes
    angle = phase.astype(np.float32) * np.float32(2.0 * math.pi / planes)
    even = (row_index % 2 == 0)[None, :]
    table = np.float32(math.sqrt(2.0 / planes)) * np.where(even, np.cos(angle), -np.sin(angle))
    return table.astype(np.float32).astype(ml_dtypes.bfloat16)


def iota(shape, dim):
    return lax.broadcasted_iota(jnp.int32, shape, dim)


def dot_f32(a, b, dims):
    return lax.dot_general(a, b, dims, precision=HP, preferred_element_type=jnp.float32)


def dot_bf16(a, b, dims=(((1,), (0,)), ((), ()))):
    return lax.dot_general(a, b, dims, preferred_element_type=jnp.float32)


def geometry_row(geo, cells, nodes):
    rows = geo.shape[0]
    spread = (iota((cells, nodes), 1) % cells == iota((cells, nodes), 0)).astype(jnp.float32)
    wide = dot_f32(geo, spread, (((1,), (0,)), ((), ())))
    own = iota((rows, nodes), 1) // cells == iota((rows, nodes), 0)
    return jnp.sum(jnp.where(own, wide, 0.0), axis=0, keepdims=True)


def slope_matrices(der, metric_r, metric_z, rows, cells, edge):
    elem = der.shape[1]
    nodes = rows * cells
    left, right = iota((nodes, nodes), 0), iota((nodes, nodes), 1)
    by_row = (iota((nodes, elem), 0) // cells == iota((nodes, elem), 1)).astype(jnp.float32)
    by_axial = (iota((nodes, elem), 0) % elem == iota((nodes, elem), 1)).astype(jnp.float32)
    radial = dot_f32(dot_f32(by_row, der[0], NT), by_row, NT)
    radial = jnp.where(left % cells == right % cells, radial, 0.0) * metric_r
    axial = dot_f32(dot_f32(by_axial, der[1], NT), by_axial, NT)
    axial = jnp.where(left // elem == right // elem, axial, 0.0) * metric_z
    following = pltpu.roll(axial, nodes - 1, 1)
    previous = pltpu.roll(axial, 1, 1)
    cell = right % cells
    last = (cell % elem == elem - 1) & (cell != cells - 1)
    first = (cell % elem == 0) & (cell != 0)
    mean = jnp.where(last, 0.5 * (axial + following), axial)
    mean = jnp.where(first, 0.5 * (axial + previous), mean)
    mean = jnp.where(cell == edge, 0.5 * axial, mean)
    return radial, mean


def fused_kernel(
    n,
    slots,
    vm,
    geo_in,
    der_in,
    loads_in,
    owner_in,
    tile_in,
    sa,
    sm_in,
    table,
    table_t,
    out,
    recv,
    rhs,
    vel,
    swirl,
    radial,
    axial,
    forcing,
    total,
    res,
    tab_v,
    tabt_v,
    sa_v,
    sm,
    geo,
    der,
    loads,
    owner,
    tile,
    scaled,
    gmat,
    load_rows,
    ids_send,
    ids_recv,
    pick_send,
    pick_recv,
    face_send,
    face_recv,
    f_send,
    f_recv,
    b_send,
    b_recv,
    small_send,
    small_recv,
    x_send,
    x_recv,
    local_sem,
):
    me = lax.axis_index("az")
    mer = lax.axis_index("mer")
    local = vm.shape[1]
    planes = table.shape[0]
    rows, cells = geo.shape[1], geo.shape[2]
    nodes = rows * cells
    jobs = sm.shape[0]
    steps = planes // CHUNK
    bf16 = jnp.bfloat16

    small = [
        pltpu.make_async_copy(owner_in, owner, local_sem.at[6]),
        pltpu.make_async_copy(tile_in, tile, local_sem.at[7]),
        pltpu.make_async_copy(loads_in, loads, local_sem.at[8]),
    ]
    loading = [
        pltpu.make_async_copy(geo_in, geo, local_sem.at[0]),
        pltpu.make_async_copy(der_in, der, local_sem.at[1]),
        pltpu.make_async_copy(sm_in.at[0, 0], sm, local_sem.at[2]),
        pltpu.make_async_copy(sa.at[0, 0], sa_v, local_sem.at[3]),
        pltpu.make_async_copy(table, tab_v, local_sem.at[4]),
        pltpu.make_async_copy(table_t, tabt_v, local_sem.at[5]),
    ]
    for copy in small + loading[:5]:
        copy.start()

    barrier = pltpu.get_barrier_semaphore()

    def greet(o, carry):
        pl.semaphore_signal(
            barrier, inc=1, device_id=(lax.rem(me + o, n), mer), device_id_type=MESH
        )
        return carry

    lax.fori_loop(1, n, greet, 0)
    pl.semaphore_signal(barrier, inc=1, device_id=(me, 1 - mer), device_id_type=MESH)

    small[0].wait()
    small[1].wait()
    job = iota((1, 128), 1) % jobs
    codes = jnp.zeros((1, 128), jnp.int32)
    tiles_per_blade = loads.shape[3] // 128
    for j in range(jobs):
        t = tile[0, 0, j]
        code = owner[t // tiles_per_blade] * tiles_per_blade + lax.rem(t, tiles_per_blade)
        codes = jnp.where(job == j, code, codes)
    ids_send[0] = codes
    ids_recv[me] = codes

    pl.semaphore_wait(barrier, n)

    def send_ids(o, carry):
        peer = lax.rem(me + o, n)
        pltpu.make_async_remote_copy(
            src_ref=ids_send.at[0],
            dst_ref=ids_recv.at[me],
            send_sem=small_send.at[0],
            recv_sem=small_recv.at[0],
            device_id=(peer, mer),
            device_id_type=MESH,
        ).start()
        return carry

    lax.fori_loop(1, n, send_ids, 0)

    def send_forward(c):
        def body(o, carry):
            peer = lax.rem(me + o, n)
            pltpu.make_async_remote_copy(
                src_ref=vm.at[c, :, pl.ds(pl.multiple_of(peer * nodes, nodes), nodes)],
                dst_ref=recv.at[c, pl.ds(pl.multiple_of(me * local, local), local), :],
                send_sem=f_send.at[c],
                recv_sem=f_recv.at[c],
                device_id=(peer, mer),
                device_id_type=MESH,
            ).start()
            return carry

        lax.fori_loop(1, n, body, 0)
        pltpu.make_async_copy(
            vm.at[c, :, pl.ds(pl.multiple_of(me * nodes, nodes), nodes)],
            recv.at[c, pl.ds(pl.multiple_of(me * local, local), local), :],
            f_recv.at[c],
        ).start()

    send_forward(0)
    send_forward(1)

    loading[0].wait()
    loading[1].wait()
    edge = (1 - mer) * (cells - 1)
    q = geometry_row(geo[0], cells, nodes)
    grad_r, grad_z = slope_matrices(
        der,
        geometry_row(geo[1], cells, nodes),
        geometry_row(geo[2], cells, nodes),
        rows,
        cells,
        edge,
    )
    for side, grad in ((0, grad_r), (1, grad_z)):
        high = grad.astype(bf16)
        low = (grad - high.astype(jnp.float32)).astype(bf16)
        at = slice(side * nodes, (side + 1) * nodes)
        gmat[0:nodes, at] = high
        gmat[nodes : 2 * nodes, at] = high
        gmat[2 * nodes : 3 * nodes, at] = low
    lane = iota((rows, nodes), 1)
    on_edge = (lane // cells == iota((rows, nodes), 0)) & (lane % cells == edge)
    take_edge = jnp.where(on_edge, 2.0, 0.0).astype(bf16)
    put_edge = jnp.where(on_edge, 0.5, 0.0).astype(bf16)

    small[2].wait()
    load_rows[...] = jnp.zeros(load_rows.shape, jnp.float32)
    for s in range(slots):
        load_rows[3 * s : 3 * s + 3, :] = loads[0, s].astype(jnp.float32)

    pltpu.make_async_copy(
        ids_recv.at[pl.ds(0, n - 1)],
        ids_recv.at[pl.ds(0, n - 1)],
        small_recv.at[0],
    ).wait()
    asked = jnp.broadcast_to(ids_recv[...], (n, 16, 128)).reshape(n * 16, 128)
    for_row = iota((n * 16, 128), 1) % jobs == iota((n * 16, 128), 0) % jobs
    asked = jnp.where(for_row, asked.astype(jnp.float32), 0.0)
    asked = jnp.max(asked, axis=1, keepdims=True).astype(jnp.int32)
    asked = jnp.broadcast_to(asked, (n * 16, 128))
    part = (iota((n * 16, 128), 0) % 16) // jobs
    slot = asked // tiles_per_blade - me * slots
    wanted = slot * 3 + part
    held = (slot >= 0) & (slot < slots) & (part < 3)
    chosen = jnp.where(held & (iota((n * 16, 128), 1) == wanted), 1.0, 0.0)
    every = dot_bf16(chosen[:, :16].astype(bf16), load_rows[...].astype(bf16))
    tile_of = lax.rem(asked, tiles_per_blade)
    picks = jnp.zeros((n * 16, 128), jnp.float32)
    for t in range(tiles_per_blade):
        picks = picks + jnp.where(tile_of == t, every[:, t * 128 : (t + 1) * 128], 0.0)
    pick_send[...] = picks.astype(bf16)
    pick_recv[pl.ds(pl.multiple_of(me * 16, 16), 16), :] = pick_send[
        pl.ds(pl.multiple_of(me * 16, 16), 16), :
    ]

    def send_picks(o, carry):
        peer = lax.rem(me + o, n)
        pltpu.make_async_remote_copy(
            src_ref=pick_send.at[pl.ds(pl.multiple_of(peer * 16, 16), 16), :],
            dst_ref=pick_recv.at[pl.ds(pl.multiple_of(me * 16, 16), 16), :],
            send_sem=small_send.at[1],
            recv_sem=small_recv.at[1],
            device_id=(peer, mer),
            device_id_type=MESH,
        ).start()
        return carry

    lax.fori_loop(1, n, send_picks, 0)
    send_forward(2)
    loading[5].start()

    def over_planes(body, unroll=False):
        def step(s, carry):
            body(pl.ds(pl.multiple_of(s * CHUNK, CHUNK), CHUNK))
            return carry

        lax.fori_loop(0, steps, step, 0, unroll=unroll)

    def arrived(c):
        pltpu.make_async_copy(recv.at[c], recv.at[c], f_recv.at[c]).wait()

    def slope_modes(c):
        wide = recv[c].astype(jnp.float32)
        index = iota((planes, nodes), 0)
        wave = (index // 2).astype(jnp.float32) * (2.0 * math.pi / planes)
        after = pltpu.roll(wide, planes - 1, 0)
        before = pltpu.roll(wide, 1, 0)
        rhs[:, nodes : 2 * nodes] = jnp.where(
            index % 2 == 0, -wave * after, wave * before
        ).astype(bf16)

    def slopes_at(c, at, u):
        high = u.astype(bf16)
        low = (u - high.astype(jnp.float32)).astype(bf16)
        slopes = dot_bf16(jnp.concatenate([high, low, high], axis=1), gmat[...])
        radial[c, at, :] = slopes[:, 0:nodes]
        sz = slopes[:, nodes : 2 * nodes]
        axial[c, at, :] = sz
        face_send[c, :, at] = dot_bf16(take_edge, sz.astype(bf16), NT)

    def face_copy(c):
        return pltpu.make_async_remote_copy(
            src_ref=face_send.at[c],
            dst_ref=face_recv.at[c],
            send_sem=x_send.at[c],
            recv_sem=x_recv.at[c],
            device_id=(me, 1 - mer),
            device_id_type=MESH,
        )

    def to_planes(c):
        arrived(c)
        slope_modes(c)
        rhs[:, 0:nodes] = recv[c]

        def body(at):
            both = dot_bf16(tab_v[at, :], rhs[...])
            u = both[:, 0:nodes]
            vel[c, at, :] = u
            swirl[c, at, :] = both[:, nodes : 2 * nodes]
            slopes_at(c, at, u)

        over_planes(body)
        face_copy(c).start()

    loading[4].wait()
    to_planes(0)
    to_planes(1)

    loading[2].wait()
    pltpu.make_async_copy(
        pick_recv.at[pl.ds(0, (n - 1) * 16), :],
        pick_recv.at[pl.ds(0, (n - 1) * 16), :],
        small_recv.at[1],
    ).wait()
    picked = jnp.sum(pick_recv[...].astype(jnp.float32).reshape(n, 16, 128), axis=0).astype(bf16)
    unit = (iota((128, 128), 0) == iota((128, 128), 1)).astype(jnp.float32).astype(bf16)
    columns = dot_bf16(unit, picked, NT)
    for j in range(jobs):
        weight = sm[j].astype(jnp.float32)
        for i in range(3):
            column = columns[:, i * jobs + j : i * jobs + j + 1]
            scaled[j * 128 : (j + 1) * 128, i * nodes : (i + 1) * nodes] = (
                column * weight
            ).astype(bf16)
    loading[3].wait()

    def force(at):
        lhs = sa_v[:, :, at].reshape(jobs * 128, CHUNK)
        forcing[at, :] = dot_bf16(lhs, scaled[...], TN)

    over_planes(force)

    for i in range(2):
        face_copy(i).wait()

    def partial(at):
        ur, ut = vel[0, at, :], vel[1, at, :]
        qt = q * ut
        for i in range(2):
            other = dot_bf16(face_recv[i, :, at].astype(bf16), put_edge, TN)
            axial[i, at, :] = axial[i, at, :] + other
            value = ur * radial[i, at, :] + qt * swirl[i, at, :]
            value = value - qt * ut if i == 0 else value + qt * ur
            radial[i, at, :] = value + forcing[at, i * nodes : (i + 1) * nodes]

    over_planes(partial)
    loading[5].wait()

    arrived(2)

    def first_terms(at):
        uz = dot_bf16(tab_v[at, :], recv[2])
        vel[2, at, :] = uz
        for i in range(2):
            total[at, i * nodes : (i + 1) * nodes] = (
                radial[i, at, :] + uz * axial[i, at, :]
            ).astype(bf16)

    over_planes(first_terms, True)

    peers = CHUNK // local
    chunk_of, seat = me // peers, lax.rem(me, peers)

    def to_modes(components):
        count, first = len(components), components[0]
        these = pl.ds(first, count)
        for k in (2, 3, 1, 0):
            chunk = lax.rem(chunk_of + k, steps)
            at = pl.ds(pl.multiple_of(chunk * CHUNK, CHUNK), CHUNK)
            back = dot_bf16(tabt_v[at, :], total[:, 0 : count * nodes])
            for d, i in enumerate(components):
                res[i, at, :] = back[:, d * nodes : (d + 1) * nodes].astype(bf16)

            def send(o, carry):
                peer = chunk * peers + lax.rem(seat + o, peers)
                pltpu.make_async_remote_copy(
                    src_ref=res.at[these, pl.ds(pl.multiple_of(peer * local, local), local), :],
                    dst_ref=out.at[these, :, pl.ds(pl.multiple_of(me * nodes, nodes), nodes)],
                    send_sem=b_send.at[first],
                    recv_sem=b_recv.at[first],
                    device_id=(peer, mer),
                    device_id_type=MESH,
                ).start()
                return carry

            lax.fori_loop(1 if k == 0 else 0, peers, send, 0)
        pltpu.make_async_copy(
            res.at[these, pl.ds(pl.multiple_of(me * local, local), local), :],
            out.at[these, :, pl.ds(pl.multiple_of(me * nodes, nodes), nodes)],
            b_recv.at[first],
        ).start()

    to_modes((0, 1))

    slope_modes(2)

    def own_slopes(at):
        swirl[2, at, :] = dot_bf16(tab_v[at, :], rhs[:, nodes : 2 * nodes])
        slopes_at(2, at, vel[2, at, :])

    over_planes(own_slopes)
    face_copy(2).start()
    face_copy(2).wait()

    def last_term(at):
        other = dot_bf16(face_recv[2, :, at].astype(bf16), put_edge, TN)
        value = vel[0, at, :] * radial[2, at, :] + vel[2, at, :] * (axial[2, at, :] + other)
        value = value + (q * vel[1, at, :]) * swirl[2, at, :]
        total[at, 0:nodes] = (value + forcing[at, 2 * nodes : 3 * nodes]).astype(bf16)

    over_planes(last_term)
    to_modes((2,))

    sent = recv.at[0, pl.ds(0, (n - 1) * local), :]
    for c in range(3):
        pltpu.make_async_copy(sent, sent, f_send.at[c]).wait()
    sent = ids_recv.at[pl.ds(0, n - 1)]
    pltpu.make_async_copy(sent, sent, small_send.at[0]).wait()
    sent = pick_recv.at[pl.ds(0, (n - 1) * 16), :]
    pltpu.make_async_copy(sent, sent, small_send.at[1]).wait()
    for first, count in ((0, 2), (2, 1)):
        sent = recv.at[pl.ds(first, count), pl.ds(0, (n - 1) * local), :]
        pltpu.make_async_copy(sent, sent, b_send.at[first]).wait()
        landed = out.at[pl.ds(first, count)]
        pltpu.make_async_copy(landed, landed, b_recv.at[first]).wait()


def on_device_fused(
    velocity_modes,
    geometry,
    derivative,
    blade_load,
    blade_owner,
    spread_tile,
    spread_azimuth,
    spread_meridional,
):
    n = lax.axis_size("az")
    local = velocity_modes.shape[1]
    planes = n * local
    rows, cells = geometry.shape[1], geometry.shape[2]
    nodes = rows * cells
    jobs = spread_tile.shape[2]
    slots = blade_load.shape[1]
    if local % 16 or planes != 4 * CHUNK or CHUNK % local or lax.axis_size("mer") != 2 or 3 * slots > 16 or jobs != 4:
        return on_device(
            velocity_modes,
            geometry,
            derivative,
            blade_load,
            blade_owner,
            spread_tile,
            spread_azimuth,
            spread_meridional,
        )
    table = host_table(planes)
    bf16, f32 = jnp.bfloat16, jnp.float32
    hbm = pl.BlockSpec(memory_space=pltpu.HBM)
    dma = pltpu.SemaphoreType.DMA
    return pl.pallas_call(
        functools.partial(fused_kernel, n, slots),
        out_shape=jax.ShapeDtypeStruct(velocity_modes.shape, bf16),
        in_specs=[hbm] * 10,
        out_specs=pl.BlockSpec(memory_space=pl.ANY),
        scratch_shapes=[
            pltpu.VMEM((3, planes, nodes), bf16),
            pltpu.VMEM((planes, 2 * nodes), bf16),
            pltpu.VMEM((3, planes, nodes), f32),
            pltpu.VMEM((3, planes, nodes), f32),
            pltpu.VMEM((3, planes, nodes), f32),
            pltpu.VMEM((3, planes, nodes), f32),
            pltpu.VMEM((planes, 3 * nodes), f32),
            pltpu.VMEM((planes, 2 * nodes), bf16),
            pltpu.VMEM((3, planes, nodes), bf16),
            pltpu.VMEM((planes, planes), bf16),
            pltpu.VMEM((planes, planes), bf16),
            pltpu.VMEM((jobs, TILE, planes), bf16),
            pltpu.VMEM((jobs, TILE, nodes), bf16),
            pltpu.VMEM(geometry.shape, f32),
            pltpu.VMEM(derivative.shape, f32),
            pltpu.VMEM(blade_load.shape, bf16),
            pltpu.SMEM(blade_owner.shape, jnp.int32),
            pltpu.SMEM(spread_tile.shape, jnp.int32),
            pltpu.VMEM((jobs * TILE, 3 * nodes), bf16),
            pltpu.VMEM((3 * nodes, 2 * nodes), bf16),
            pltpu.VMEM((16, blade_load.shape[3]), f32),
            pltpu.VMEM((1, 1, 128), jnp.int32),
            pltpu.VMEM((n, 1, 128), jnp.int32),
            pltpu.VMEM((n * 16, 128), bf16),
            pltpu.VMEM((n * 16, 128), bf16),
            pltpu.VMEM((3, rows, planes), f32),
            pltpu.VMEM((3, rows, planes), f32),
            dma((3,)),
            dma((3,)),
            dma((3,)),
            dma((3,)),
            dma((2,)),
            dma((2,)),
            dma((3,)),
            dma((3,)),
            dma((9,)),
        ],
        compiler_params=pltpu.CompilerParams(
            collective_id=0, has_side_effects=True, vmem_limit_bytes=60 * 1024 * 1024
        ),
    )(
        velocity_modes,
        geometry,
        derivative,
        blade_load,
        blade_owner,
        spread_tile,
        spread_azimuth,
        spread_meridional,
        jnp.asarray(table),
        jnp.asarray(np.ascontiguousarray(table.T)),
    )


def solution(mesh):
    in_specs = (
        P(None, "az", "mer"),
        P(None, "az", "mer"),
        P(),
        P("az", None, None, None),
        P(),
        P("mer", "az", None),
        P("mer", "az", None, None, None),
        P("mer", "az", None, None, None),
    )
    out_specs = P(None, "az", "mer")
    return jax.shard_map(
        on_device_fused, mesh=mesh, in_specs=in_specs, out_specs=out_specs, check_vma=False
    )
```

```python
import functools
import math

import jax
import jax.numpy as jnp
import ml_dtypes
import numpy as np
from jax import lax
from jax.experimental import pallas as pl
from jax.experimental.pallas import tpu as pltpu
from jax.sharding import PartitionSpec as P

PLANES = 1024
TILE = 128


def extended(shard, sides, width):
    for axis, dim in sides:
        count, length = (lax.axis_size(axis), shard.shape[dim])
        up = [(i, (i + 1) % count) for i in range(count - 1)]
        down = [(j, i) for i, j in up]
        last = lax.slice_in_dim(shard, length - width, length, axis=dim)
        leading = lax.slice_in_dim(shard, 0, width, axis=dim)
        before = lax.ppermute(last, axis, up)
        after = lax.ppermute(leading, axis, down)
        shard = jnp.concatenate([before, shard, after], axis=dim)
    return shard


def make_table(planes):
    row_index = jnp.arange(planes, dtype=jnp.int32)
    wave_index = row_index // 2
    phase_index = row_index[:, None] * wave_index[None, :] % planes
    angle_rad = phase_index.astype(jnp.float32) * (2.0 * math.pi / planes)
    even_rows = (row_index % 2 == 0)[None, :]
    dft_table = math.sqrt(2.0 / planes) * jnp.where(
        even_rows, jnp.cos(angle_rad), -jnp.sin(angle_rad)
    )
    return dft_table.astype(jnp.bfloat16)


def slope_of(mode_block, first_pair, planes):
    shape_all = mode_block.shape
    mode_pairs = mode_block.reshape(shape_all[0], shape_all[1] // 2, 2, shape_all[2]).astype(
        jnp.float32
    )
    wave_number = (first_pair + jnp.arange(shape_all[1] // 2, dtype=jnp.int32)).astype(
        jnp.float32
    ) * (2.0 * math.pi / planes)
    wave_number = wave_number[None, :, None]
    result = jnp.stack(
        [-wave_number * mode_pairs[:, :, 1], wave_number * mode_pairs[:, :, 0]], axis=2
    )
    return result.reshape(shape_all).astype(jnp.bfloat16)


def inverse_of(dft_table, mode_block):
    return jnp.einsum("pj,cjn->cpn", dft_table, mode_block, preferred_element_type=jnp.float32)


def slopes_of(velocity, geometry, derivative):
    hp = lax.Precision.HIGHEST
    shape_all = velocity.shape
    elem_size = derivative.shape[1]
    elements = shape_all[3] // elem_size
    radial_slope = geometry[1] * jnp.einsum("rs,cpsz->cprz", derivative[0], velocity, precision=hp)
    blocks = velocity.reshape(shape_all[0], shape_all[1], shape_all[2], elements, elem_size)
    raw_slope = jnp.einsum("at,cpret->cprea", derivative[1], blocks, precision=hp)
    axial_slope = raw_slope * geometry[2].reshape(shape_all[2], elements, elem_size)
    first_face = axial_slope[..., 0]
    last_face = axial_slope[..., elem_size - 1]
    face_mean = 0.5 * (last_face[..., :-1] + first_face[..., 1:])
    new_first = first_face.at[..., 1:].set(face_mean)
    new_last = last_face.at[..., :-1].set(face_mean)
    return (radial_slope, axial_slope, first_face, last_face, new_first, new_last)


def advect(velocity, radial_slope, axial_slope, swirl_slope, inverse_radius):
    radial_vel = velocity[0]
    swirl_vel = velocity[1]
    axial_vel = velocity[2]
    advection = (
        radial_vel[None] * radial_slope
        + axial_vel[None] * axial_slope
        + (inverse_radius * swirl_vel)[None] * swirl_slope
    )
    advection = advection.at[0].add(-(inverse_radius * swirl_vel * swirl_vel))
    advection = advection.at[1].add(inverse_radius * radial_vel * swirl_vel)
    return advection


def forcing_of(all_loads, tile_ids, spread_az, spread_mer, tile_size):
    blades = all_loads.shape[0]
    tiles_count = all_loads.shape[2] // tile_size
    tile_loads = (
        all_loads.reshape(blades, 3, tiles_count, tile_size)
        .transpose(0, 2, 1, 3)
        .reshape(blades * tiles_count, 3, tile_size)
    )
    picked = jnp.take(tile_loads, tile_ids, axis=0)
    scaled = (
        picked.astype(jnp.float32)[:, :, :, None] * spread_mer.astype(jnp.float32)[:, None, :, :]
    ).astype(jnp.bfloat16)
    return jnp.einsum("jmp,jcmn->cpn", spread_az, scaled, preferred_element_type=jnp.float32)


def on_device(
    velocity_modes,
    geometry,
    derivative,
    blade_load,
    blade_owner,
    spread_tile,
    spread_azimuth,
    spread_meridional,
):
    planes = PLANES
    dft_table = make_table(planes)
    local_modes = velocity_modes.shape[1]
    block_cells = geometry.shape[1] * geometry.shape[2]
    first_pair = lax.axis_index("az") * (local_modes // 2)
    slope_local = slope_of(velocity_modes, first_pair, planes)
    velocity = inverse_of(
        dft_table, lax.all_to_all(velocity_modes, "az", split_axis=2, concat_axis=1, tiled=True)
    )
    swirl_slope = inverse_of(
        dft_table, lax.all_to_all(slope_local, "az", split_axis=2, concat_axis=1, tiled=True)
    )
    rows = geometry.shape[1]
    cells = geometry.shape[2]
    velocity = velocity.reshape(3, planes, rows, cells)
    swirl_slope = swirl_slope.reshape(3, planes, rows, cells)
    radial_slope, axial_slope, first_face, last_face, new_first, new_last = slopes_of(
        velocity, geometry, derivative
    )
    edge_values = jnp.stack([first_face[..., 0], last_face[..., -1]], axis=-1)
    padded = extended(edge_values.astype(jnp.bfloat16), (("mer", 3),), 1).astype(edge_values.dtype)
    mer_index = lax.axis_index("mer")
    mer_count = lax.axis_size("mer")
    left_value = jnp.where(
        mer_index > 0, 0.5 * (padded[..., 0] + first_face[..., 0]), first_face[..., 0]
    )
    right_value = jnp.where(
        mer_index < mer_count - 1, 0.5 * (last_face[..., -1] + padded[..., 3]), last_face[..., -1]
    )
    new_first = new_first.at[..., 0].set(left_value)
    new_last = new_last.at[..., -1].set(right_value)
    elem_size = derivative.shape[1]
    axial_slope = axial_slope.at[..., 0].set(new_first).at[..., elem_size - 1].set(new_last)
    axial_slope = axial_slope.reshape(3, planes, rows, cells)
    advection = advect(velocity, radial_slope, axial_slope, swirl_slope, geometry[0])
    local_slots = blade_load[0]
    every_slot = lax.all_gather(blade_load, "az", axis=0, tiled=True)
    all_loads = every_slot.reshape(-1, 3, local_slots.shape[2])[blade_owner]
    forcing = forcing_of(
        all_loads, spread_tile[0, 0], spread_azimuth[0, 0], spread_meridional[0, 0], TILE
    )
    total_term = (advection.reshape(3, planes, block_cells) + forcing).astype(jnp.bfloat16)
    result = jnp.einsum(
        "pj,cpn->cjn", dft_table, total_term, preferred_element_type=jnp.float32
    ).astype(jnp.bfloat16)
    return lax.all_to_all(result, "az", split_axis=1, concat_axis=2, tiled=True)


CHUNK = 256
MESH = pl.DeviceIdType.MESH
HP = lax.Precision.HIGHEST
NT = (((1,), (1,)), ((), ()))
TN = (((0,), (0,)), ((), ()))


def host_table(planes):
    row_index = np.arange(planes, dtype=np.int32)
    phase = (row_index[:, None] * (row_index // 2)[None, :]) % planes
    angle = phase.astype(np.float32) * np.float32(2.0 * math.pi / planes)
    even = (row_index % 2 == 0)[None, :]
    table = np.float32(math.sqrt(2.0 / planes)) * np.where(even, np.cos(angle), -np.sin(angle))
    return table.astype(np.float32).astype(ml_dtypes.bfloat16)


def iota(shape, dim):
    return lax.broadcasted_iota(jnp.int32, shape, dim)


def dot_f32(a, b, dims):
    return lax.dot_general(a, b, dims, precision=HP, preferred_element_type=jnp.float32)


def dot_bf16(a, b, dims=(((1,), (0,)), ((), ()))):
    return lax.dot_general(a, b, dims, preferred_element_type=jnp.float32)


def geometry_row(geo, cells, nodes):
    rows = geo.shape[0]
    spread = (iota((cells, nodes), 1) % cells == iota((cells, nodes), 0)).astype(jnp.float32)
    wide = dot_f32(geo, spread, (((1,), (0,)), ((), ())))
    own = iota((rows, nodes), 1) // cells == iota((rows, nodes), 0)
    return jnp.sum(jnp.where(own, wide, 0.0), axis=0, keepdims=True)


def slope_matrices(der, metric_r, metric_z, rows, cells, edge):
    elem = der.shape[1]
    nodes = rows * cells
    left, right = iota((nodes, nodes), 0), iota((nodes, nodes), 1)
    by_row = (iota((nodes, elem), 0) // cells == iota((nodes, elem), 1)).astype(jnp.float32)
    by_axial = (iota((nodes, elem), 0) % elem == iota((nodes, elem), 1)).astype(jnp.float32)
    radial = dot_f32(dot_f32(by_row, der[0], NT), by_row, NT)
    radial = jnp.where(left % cells == right % cells, radial, 0.0) * metric_r
    axial = dot_f32(dot_f32(by_axial, der[1], NT), by_axial, NT)
    axial = jnp.where(left // elem == right // elem, axial, 0.0) * metric_z
    following = pltpu.roll(axial, nodes - 1, 1)
    previous = pltpu.roll(axial, 1, 1)
    cell = right % cells
    last = (cell % elem == elem - 1) & (cell != cells - 1)
    first = (cell % elem == 0) & (cell != 0)
    mean = jnp.where(last, 0.5 * (axial + following), axial)
    mean = jnp.where(first, 0.5 * (axial + previous), mean)
    mean = jnp.where(cell == edge, 0.5 * axial, mean)
    return radial, mean


def fused_kernel(
    n,
    slots,
    vm,
    geo_in,
    der_in,
    loads_in,
    owner_in,
    tile_in,
    sa,
    sm_in,
    table,
    table_t,
    out,
    recv,
    rhs,
    vel,
    swirl,
    radial,
    axial,
    forcing,
    total,
    res,
    tab_v,
    tabt_v,
    sa_v,
    sm,
    geo,
    der,
    loads,
    owner,
    tile,
    scaled,
    gmat,
    load_rows,
    ids_send,
    ids_recv,
    pick_send,
    pick_recv,
    face_send,
    face_recv,
    f_send,
    f_recv,
    b_send,
    b_recv,
    small_send,
    small_recv,
    x_send,
    x_recv,
    local_sem,
):
    me = lax.axis_index("az")
    mer = lax.axis_index("mer")
    local = vm.shape[1]
    planes = table.shape[0]
    rows, cells = geo.shape[1], geo.shape[2]
    nodes = rows * cells
    jobs = sm.shape[0]
    steps = planes // CHUNK
    bf16 = jnp.bfloat16

    small = [
        pltpu.make_async_copy(owner_in, owner, local_sem.at[6]),
        pltpu.make_async_copy(tile_in, tile, local_sem.at[7]),
        pltpu.make_async_copy(loads_in, loads, local_sem.at[8]),
    ]
    loading = [
        pltpu.make_async_copy(geo_in, geo, local_sem.at[0]),
        pltpu.make_async_copy(der_in, der, local_sem.at[1]),
        pltpu.make_async_copy(sm_in.at[0, 0], sm, local_sem.at[2]),
        pltpu.make_async_copy(sa.at[0, 0], sa_v, local_sem.at[3]),
        pltpu.make_async_copy(table, tab_v, local_sem.at[4]),
        pltpu.make_async_copy(table_t, tabt_v, local_sem.at[5]),
    ]
    for copy in small + loading[:5]:
        copy.start()

    barrier = pltpu.get_barrier_semaphore()

    def greet(o, carry):
        pl.semaphore_signal(
            barrier, inc=1, device_id=(lax.rem(me + o, n), mer), device_id_type=MESH
        )
        return carry

    lax.fori_loop(1, n, greet, 0)
    pl.semaphore_signal(barrier, inc=1, device_id=(me, 1 - mer), device_id_type=MESH)

    small[0].wait()
    small[1].wait()
    job = iota((1, 128), 1) % jobs
    codes = jnp.zeros((1, 128), jnp.int32)
    tiles_per_blade = loads.shape[3] // 128
    for j in range(jobs):
        t = tile[0, 0, j]
        code = owner[t // tiles_per_blade] * tiles_per_blade + lax.rem(t, tiles_per_blade)
        codes = jnp.where(job == j, code, codes)
    ids_send[0] = codes
    ids_recv[me] = codes

    pl.semaphore_wait(barrier, n)

    def send_ids(o, carry):
        peer = lax.rem(me + o, n)
        pltpu.make_async_remote_copy(
            src_ref=ids_send.at[0],
            dst_ref=ids_recv.at[me],
            send_sem=small_send.at[0],
            recv_sem=small_recv.at[0],
            device_id=(peer, mer),
            device_id_type=MESH,
        ).start()
        return carry

    lax.fori_loop(1, n, send_ids, 0)

    def send_forward(c):
        def body(o, carry):
            peer = lax.rem(me + o, n)
            pltpu.make_async_remote_copy(
                src_ref=vm.at[c, :, pl.ds(pl.multiple_of(peer * nodes, nodes), nodes)],
                dst_ref=recv.at[c, pl.ds(pl.multiple_of(me * local, local), local), :],
                send_sem=f_send.at[c],
                recv_sem=f_recv.at[c],
                device_id=(peer, mer),
                device_id_type=MESH,
            ).start()
            return carry

        lax.fori_loop(1, n, body, 0)
        pltpu.make_async_copy(
            vm.at[c, :, pl.ds(pl.multiple_of(me * nodes, nodes), nodes)],
            recv.at[c, pl.ds(pl.multiple_of(me * local, local), local), :],
            f_recv.at[c],
        ).start()

    send_forward(0)
    send_forward(1)

    loading[0].wait()
    loading[1].wait()
    edge = (1 - mer) * (cells - 1)
    q = geometry_row(geo[0], cells, nodes)
    grad_r, grad_z = slope_matrices(
        der,
        geometry_row(geo[1], cells, nodes),
        geometry_row(geo[2], cells, nodes),
        rows,
        cells,
        edge,
    )
    for side, grad in ((0, grad_r), (1, grad_z)):
        high = grad.astype(bf16)
        low = (grad - high.astype(jnp.float32)).astype(bf16)
        at = slice(side * nodes, (side + 1) * nodes)
        gmat[0:nodes, at] = high
        gmat[nodes : 2 * nodes, at] = high
        gmat[2 * nodes : 3 * nodes, at] = low
    lane = iota((rows, nodes), 1)
    on_edge = (lane // cells == iota((rows, nodes), 0)) & (lane % cells == edge)
    take_edge = jnp.where(on_edge, 2.0, 0.0).astype(bf16)
    put_edge = jnp.where(on_edge, 0.5, 0.0).astype(bf16)

    small[2].wait()
    load_rows[...] = jnp.zeros(load_rows.shape, jnp.float32)
    for s in range(slots):
        load_rows[3 * s : 3 * s + 3, :] = loads[0, s].astype(jnp.float32)

    pltpu.make_async_copy(
        ids_recv.at[pl.ds(0, n - 1)],
        ids_recv.at[pl.ds(0, n - 1)],
        small_recv.at[0],
    ).wait()
    asked = jnp.broadcast_to(ids_recv[...], (n, 16, 128)).reshape(n * 16, 128)
    for_row = iota((n * 16, 128), 1) % jobs == iota((n * 16, 128), 0) % jobs
    asked = jnp.where(for_row, asked.astype(jnp.float32), 0.0)
    asked = jnp.max(asked, axis=1, keepdims=True).astype(jnp.int32)
    asked = jnp.broadcast_to(asked, (n * 16, 128))
    part = (iota((n * 16, 128), 0) % 16) // jobs
    slot = asked // tiles_per_blade - me * slots
    wanted = slot * 3 + part
    held = (slot >= 0) & (slot < slots) & (part < 3)
    chosen = jnp.where(held & (iota((n * 16, 128), 1) == wanted), 1.0, 0.0)
    every = dot_bf16(chosen[:, :16].astype(bf16), load_rows[...].astype(bf16))
    tile_of = lax.rem(asked, tiles_per_blade)
    picks = jnp.zeros((n * 16, 128), jnp.float32)
    for t in range(tiles_per_blade):
        picks = picks + jnp.where(tile_of == t, every[:, t * 128 : (t + 1) * 128], 0.0)
    pick_send[...] = picks.astype(bf16)
    pick_recv[pl.ds(pl.multiple_of(me * 16, 16), 16), :] = pick_send[
        pl.ds(pl.multiple_of(me * 16, 16), 16), :
    ]

    def send_picks(o, carry):
        peer = lax.rem(me + o, n)
        pltpu.make_async_remote_copy(
            src_ref=pick_send.at[pl.ds(pl.multiple_of(peer * 16, 16), 16), :],
            dst_ref=pick_recv.at[pl.ds(pl.multiple_of(me * 16, 16), 16), :],
            send_sem=small_send.at[1],
            recv_sem=small_recv.at[1],
            device_id=(peer, mer),
            device_id_type=MESH,
        ).start()
        return carry

    lax.fori_loop(1, n, send_picks, 0)
    send_forward(2)
    loading[5].start()

    def over_planes(body, unroll=True):
        def step(s, carry):
            body(pl.ds(pl.multiple_of(s * CHUNK, CHUNK), CHUNK))
            return carry

        lax.fori_loop(0, steps, step, 0, unroll=unroll)

    def arrived(c):
        pltpu.make_async_copy(recv.at[c], recv.at[c], f_recv.at[c]).wait()

    def slope_modes(c):
        wide = recv[c].astype(jnp.float32)
        index = iota((planes, nodes), 0)
        wave = (index // 2).astype(jnp.float32) * (2.0 * math.pi / planes)
        after = pltpu.roll(wide, planes - 1, 0)
        before = pltpu.roll(wide, 1, 0)
        rhs[:, nodes : 2 * nodes] = jnp.where(
            index % 2 == 0, -wave * after, wave * before
        ).astype(bf16)

    def slopes_at(c, at, u):
        high = u.astype(bf16)
        low = (u - high.astype(jnp.float32)).astype(bf16)
        slopes = dot_bf16(jnp.concatenate([high, low, high], axis=1), gmat[...])
        radial[c, at, :] = slopes[:, 0:nodes]
        sz = slopes[:, nodes : 2 * nodes]
        axial[c, at, :] = sz
        face_send[c, :, at] = dot_bf16(take_edge, sz.astype(bf16), NT)

    def face_copy(c):
        return pltpu.make_async_remote_copy(
            src_ref=face_send.at[c],
            dst_ref=face_recv.at[c],
            send_sem=x_send.at[c],
            recv_sem=x_recv.at[c],
            device_id=(me, 1 - mer),
            device_id_type=MESH,
        )

    def to_planes(c):
        arrived(c)
        slope_modes(c)
        rhs[:, 0:nodes] = recv[c]

        def body(at):
            both = dot_bf16(tab_v[at, :], rhs[...])
            u = both[:, 0:nodes]
            vel[c, at, :] = u
            swirl[c, at, :] = both[:, nodes : 2 * nodes]
            slopes_at(c, at, u)

        over_planes(body)
        face_copy(c).start()

    loading[4].wait()
    to_planes(0)
    to_planes(1)

    loading[2].wait()
    pltpu.make_async_copy(
        pick_recv.at[pl.ds(0, (n - 1) * 16), :],
        pick_recv.at[pl.ds(0, (n - 1) * 16), :],
        small_recv.at[1],
    ).wait()
    picked = jnp.sum(pick_recv[...].astype(jnp.float32).reshape(n, 16, 128), axis=0).astype(bf16)
    unit = (iota((128, 128), 0) == iota((128, 128), 1)).astype(jnp.float32).astype(bf16)
    columns = dot_bf16(unit, picked, NT)
    for j in range(jobs):
        weight = sm[j].astype(jnp.float32)
        for i in range(3):
            column = columns[:, i * jobs + j : i * jobs + j + 1]
            scaled[j * 128 : (j + 1) * 128, i * nodes : (i + 1) * nodes] = (
                column * weight
            ).astype(bf16)
    loading[3].wait()

    def force(at):
        lhs = sa_v[:, :, at].reshape(jobs * 128, CHUNK)
        forcing[at, :] = dot_bf16(lhs, scaled[...], TN)

    over_planes(force)

    def partial(at):
        ur, ut = vel[0, at, :], vel[1, at, :]
        qt = q * ut
        for i in range(2):
            value = ur * radial[i, at, :] + qt * swirl[i, at, :]
            value = value - qt * ut if i == 0 else value + qt * ur
            radial[i, at, :] = value + forcing[at, i * nodes : (i + 1) * nodes]

    over_planes(partial)
    loading[5].wait()

    for i in range(2):
        face_copy(i).wait()

    def add_faces(at):
        for i in range(2):
            other = dot_bf16(face_recv[i, :, at].astype(bf16), put_edge, TN)
            axial[i, at, :] = axial[i, at, :] + other

    over_planes(add_faces)
    arrived(2)

    def first_terms(at):
        uz = dot_bf16(tab_v[at, :], recv[2])
        vel[2, at, :] = uz
        for i in range(2):
            total[at, i * nodes : (i + 1) * nodes] = (
                radial[i, at, :] + uz * axial[i, at, :]
            ).astype(bf16)

    over_planes(first_terms, True)

    peers = CHUNK // local
    chunk_of, seat = me // peers, lax.rem(me, peers)

    def to_modes(components):
        count, first = len(components), components[0]
        these = pl.ds(first, count)
        for k in (2, 3, 1, 0):
            chunk = lax.rem(chunk_of + k, steps)
            at = pl.ds(pl.multiple_of(chunk * CHUNK, CHUNK), CHUNK)
            back = dot_bf16(tabt_v[at, :], total[:, 0 : count * nodes])
            for d, i in enumerate(components):
                res[i, at, :] = back[:, d * nodes : (d + 1) * nodes].astype(bf16)

            def send(o, carry):
                peer = chunk * peers + lax.rem(seat + o, peers)
                pltpu.make_async_remote_copy(
                    src_ref=res.at[these, pl.ds(pl.multiple_of(peer * local, local), local), :],
                    dst_ref=out.at[these, :, pl.ds(pl.multiple_of(me * nodes, nodes), nodes)],
                    send_sem=b_send.at[first],
                    recv_sem=b_recv.at[first],
                    device_id=(peer, mer),
                    device_id_type=MESH,
                ).start()
                return carry

            lax.fori_loop(1 if k == 0 else 0, peers, send, 0)
        pltpu.make_async_copy(
            res.at[these, pl.ds(pl.multiple_of(me * local, local), local), :],
            out.at[these, :, pl.ds(pl.multiple_of(me * nodes, nodes), nodes)],
            b_recv.at[first],
        ).start()

    to_modes((0, 1))

    slope_modes(2)

    def own_slopes(at):
        swirl[2, at, :] = dot_bf16(tab_v[at, :], rhs[:, nodes : 2 * nodes])
        slopes_at(2, at, vel[2, at, :])

    over_planes(own_slopes)
    face_copy(2).start()
    face_copy(2).wait()

    def last_term(at):
        other = dot_bf16(face_recv[2, :, at].astype(bf16), put_edge, TN)
        value = vel[0, at, :] * radial[2, at, :] + vel[2, at, :] * (axial[2, at, :] + other)
        value = value + (q * vel[1, at, :]) * swirl[2, at, :]
        total[at, 0:nodes] = (value + forcing[at, 2 * nodes : 3 * nodes]).astype(bf16)

    over_planes(last_term)
    to_modes((2,))

    sent = recv.at[0, pl.ds(0, (n - 1) * local), :]
    for c in range(3):
        pltpu.make_async_copy(sent, sent, f_send.at[c]).wait()
    sent = ids_recv.at[pl.ds(0, n - 1)]
    pltpu.make_async_copy(sent, sent, small_send.at[0]).wait()
    sent = pick_recv.at[pl.ds(0, (n - 1) * 16), :]
    pltpu.make_async_copy(sent, sent, small_send.at[1]).wait()
    for first, count in ((0, 2), (2, 1)):
        sent = recv.at[pl.ds(first, count), pl.ds(0, (n - 1) * local), :]
        pltpu.make_async_copy(sent, sent, b_send.at[first]).wait()
        landed = out.at[pl.ds(first, count)]
        pltpu.make_async_copy(landed, landed, b_recv.at[first]).wait()


def on_device_fused(
    velocity_modes,
    geometry,
    derivative,
    blade_load,
    blade_owner,
    spread_tile,
    spread_azimuth,
    spread_meridional,
):
    n = lax.axis_size("az")
    local = velocity_modes.shape[1]
    planes = n * local
    rows, cells = geometry.shape[1], geometry.shape[2]
    nodes = rows * cells
    jobs = spread_tile.shape[2]
    slots = blade_load.shape[1]
    if local % 16 or planes != 4 * CHUNK or CHUNK % local or lax.axis_size("mer") != 2 or 3 * slots > 16 or jobs != 4:
        return on_device(
            velocity_modes,
            geometry,
            derivative,
            blade_load,
            blade_owner,
            spread_tile,
            spread_azimuth,
            spread_meridional,
        )
    table = host_table(planes)
    bf16, f32 = jnp.bfloat16, jnp.float32
    hbm = pl.BlockSpec(memory_space=pltpu.HBM)
    dma = pltpu.SemaphoreType.DMA
    return pl.pallas_call(
        functools.partial(fused_kernel, n, slots),
        out_shape=jax.ShapeDtypeStruct(velocity_modes.shape, bf16),
        in_specs=[hbm] * 10,
        out_specs=pl.BlockSpec(memory_space=pl.ANY),
        scratch_shapes=[
            pltpu.VMEM((3, planes, nodes), bf16),
            pltpu.VMEM((planes, 2 * nodes), bf16),
            pltpu.VMEM((3, planes, nodes), f32),
            pltpu.VMEM((3, planes, nodes), f32),
            pltpu.VMEM((3, planes, nodes), f32),
            pltpu.VMEM((3, planes, nodes), f32),
            pltpu.VMEM((planes, 3 * nodes), f32),
            pltpu.VMEM((planes, 2 * nodes), bf16),
            pltpu.VMEM((3, planes, nodes), bf16),
            pltpu.VMEM((planes, planes), bf16),
            pltpu.VMEM((planes, planes), bf16),
            pltpu.VMEM((jobs, TILE, planes), bf16),
            pltpu.VMEM((jobs, TILE, nodes), bf16),
            pltpu.VMEM(geometry.shape, f32),
            pltpu.VMEM(derivative.shape, f32),
            pltpu.VMEM(blade_load.shape, bf16),
            pltpu.SMEM(blade_owner.shape, jnp.int32),
            pltpu.SMEM(spread_tile.shape, jnp.int32),
            pltpu.VMEM((jobs * TILE, 3 * nodes), bf16),
            pltpu.VMEM((3 * nodes, 2 * nodes), bf16),
            pltpu.VMEM((16, blade_load.shape[3]), f32),
            pltpu.VMEM((1, 1, 128), jnp.int32),
            pltpu.VMEM((n, 1, 128), jnp.int32),
            pltpu.VMEM((n * 16, 128), bf16),
            pltpu.VMEM((n * 16, 128), bf16),
            pltpu.VMEM((3, rows, planes), f32),
            pltpu.VMEM((3, rows, planes), f32),
            dma((3,)),
            dma((3,)),
            dma((3,)),
            dma((3,)),
            dma((2,)),
            dma((2,)),
            dma((3,)),
            dma((3,)),
            dma((9,)),
        ],
        compiler_params=pltpu.CompilerParams(
            collective_id=0, has_side_effects=True, vmem_limit_bytes=60 * 1024 * 1024
        ),
    )(
        velocity_modes,
        geometry,
        derivative,
        blade_load,
        blade_owner,
        spread_tile,
        spread_azimuth,
        spread_meridional,
        jnp.asarray(table),
        jnp.asarray(np.ascontiguousarray(table.T)),
    )


def solution(mesh):
    in_specs = (
        P(None, "az", "mer"),
        P(None, "az", "mer"),
        P(),
        P("az", None, None, None),
        P(),
        P("mer", "az", None),
        P("mer", "az", None, None, None),
        P("mer", "az", None, None, None),
    )
    out_specs = P(None, "az", "mer")
    return jax.shard_map(
        on_device_fused, mesh=mesh, in_specs=in_specs, out_specs=out_specs, check_vma=False
    )
```
